32 devices in a mesh: seq: 16 (over z, y, x), head: 2 (over core).
Axes of the slice: x: 2, y: 2, z: 4, core: 2. Of those that a mesh axis runs over, the one named last changes fastest.
Arguments:
- video_query: bfloat16 [8192, 3072], P('seq', 'head'), as said below
- video_value: bfloat16 [8192, 3072], P('seq', 'head'), may hold values from -12 to 12
- audio_key: bfloat16 [4096, 3072], P('seq', 'head'), as said below
- audio_value: bfloat16 [4096, 3072], P('seq', 'head'), may hold values from -12 to 12
- video_proj: bfloat16 [3072, 3072], P('head'), may hold values from -0.109375 to 0.109375
- audio_proj: bfloat16 [3072, 3072], P('head'), may hold values from -0.109375 to 0.109375
- pair_first: int32 [16], replicated, may hold values from 0 to 15, as said below
- pair_count: int32 [16], replicated, may hold values from 1 to 5, as said below
Outputs:
- video_out: bfloat16 [8192, 3072], P('seq', 'head')
- audio_out: bfloat16 [4096, 3072], P('seq', 'head')
The draws below stay inside these ranges and needn't reach their ends.
Inputs may be any that keep to these rules, and one draw needn't show every extreme that they name: Video block b pairs with the audio blocks pair_first[b] to pair_first[b] + pair_count[b] - 1; these lie within b - 2 to b + 2, inside 0 to 15, and always include block b. `pair_count`: some video block pairs with 5 audio blocks in every draw. `video_query`: entries lie within -8 to 8. `audio_key`: entries lie within -8 to 8.
All inputs are finite; a program needn't handle non-finite values.
Results may differ from the reference program's by a relative error of at most 0.0052.
Values may be sent and summed in bfloat16 or wider, within the bound.
A program may use at most 192 MiB of HBM per device.

```python
import math
import jax
import jax.numpy as jnp
from jax import lax

D = 3072
HEADS = 24
HEAD_DIM = 128
VID_DEV = 512
AUD_DEV = 256
HALF = 2
NB = 16
C = 3072
VTOK = 8192
ATOK = 4096
N_SEQ = 16


def pair_window(key):
    window_key = jax.random.fold_in(key, 21)
    left = jax.random.randint(window_key, (NB,), 0, HALF + 1)
    right = jax.random.randint(jax.random.fold_in(window_key, 1), (NB,), 0, HALF + 1)
    blocks = jnp.arange(NB, dtype=jnp.int32)
    middle = blocks == NB // 2
    left = jnp.where(middle, HALF, left)
    right = jnp.where(middle, HALF, right)
    left = jnp.where(blocks == NB - 1, 0, left)
    right = jnp.where(blocks == 0, 0, right)
    first = jnp.maximum(blocks - left, 0)
    last = jnp.minimum(blocks + right, NB - 1)
    return (first.astype(jnp.int32), (last - first + 1).astype(jnp.int32))


def draw_video_query(key, part):
    key = jax.random.fold_in(key, 1)
    base = 1.5 * jax.random.normal(key, (VTOK, HEADS * HEAD_DIM), jnp.float32)
    return jnp.clip(base, -8.0, 8.0).astype(jnp.bfloat16)


def draw_audio_key(key, part):
    key = jax.random.fold_in(key, 2)
    base = 1.5 * jax.random.normal(key, (ATOK, HEADS * HEAD_DIM), jnp.float32)
    return jnp.clip(base, -8.0, 8.0).astype(jnp.bfloat16)


def draw_pair_first(key, part):
    first, count = pair_window(key)
    return first


def draw_pair_count(key, part):
    first, count = pair_window(key)
    return count


def levels(rng, dims, split, low, largest):
    loudness, own = 1.0, jax.random.fold_in(rng, 6)
    for position, parts in split:
        steps = jnp.exp(jax.random.uniform(jax.random.fold_in(own, position), (parts,), jnp.float32, low / len(split), largest / len(split)))
        loudness = loudness * jnp.repeat(steps, dims[position] // parts).reshape([-1 if axis == position else 1 for axis in range(len(dims))])
    return loudness


def normal_values(stream_key, extent, deviation, limit, cuts=(), held_as=jnp.bfloat16):
    entries = deviation * jax.random.normal(stream_key, extent, jnp.float32)
    if cuts:
        entries = entries * levels(stream_key, extent, cuts, -0.22, 0.18)
    return jnp.clip(entries, -limit, limit).astype(held_as)


def setup_inputs(seed: int = 0) -> dict:
    key_of = jax.random.split(jax.random.key(seed), 9)
    return {
        "video_query": draw_video_query(jax.random.fold_in(key_of[8], 71), 0),
        "video_value": normal_values(key_of[1], (VTOK, C), 2.0, 12.0, ((0, 16), (1, 2))),
        "audio_key": draw_audio_key(jax.random.fold_in(key_of[8], 71), 0),
        "audio_value": normal_values(key_of[3], (ATOK, C), 2.0, 12.0, ((0, 16), (1, 2))),
        "video_proj": normal_values(key_of[4], (C, D), C ** -0.5, 0.109375, ((0, 2),)),
        "audio_proj": normal_values(key_of[5], (C, D), C ** -0.5, 0.109375, ((0, 2),)),
        "pair_first": draw_pair_first(jax.random.fold_in(key_of[8], 71), 0),
        "pair_count": draw_pair_count(jax.random.fold_in(key_of[8], 71), 0),
    }


NEG = -1e+30

def tile_scores(query, keys):
    return jnp.einsum('vhe,ahe->hva', query.astype(jnp.float32), keys.astype(jnp.float32)) / math.sqrt(HEAD_DIM)

def row_piece(scores, values):
    top = lax.optimization_barrier(jnp.max(scores, axis=2))
    expo = jnp.exp(scores - top[:, :, None])
    total = lax.optimization_barrier(jnp.sum(expo, axis=2))
    weights = expo.astype(jnp.bfloat16)
    out = jnp.einsum('hva,ahe->vhe', weights.astype(jnp.float32), values.astype(jnp.float32))
    return (top, total, out)

def col_piece(scores, values):
    top = lax.optimization_barrier(jnp.max(scores, axis=1))
    expo = jnp.exp(scores - top[:, None, :])
    total = lax.optimization_barrier(jnp.sum(expo, axis=1))
    weights = expo.astype(jnp.bfloat16)
    out = jnp.einsum('hva,vhe->ahe', weights.astype(jnp.float32), values.astype(jnp.float32))
    return (top, total, out)

def masked(part, valid):
    top, total, out = part
    return (jnp.where(valid, top, NEG), jnp.where(valid, total, 0.0), jnp.where(valid, out, 0.0))

def combine(acc, part):
    top_a, total_a, out_a = acc
    top_b, total_b, out_b = part
    top = jnp.maximum(top_a, top_b)
    old = jnp.exp(top_a - top)
    new = jnp.exp(top_b - top)
    return (top, total_a * old + total_b * new, out_a * old.T[:, :, None] + out_b * new.T[:, :, None])

def empty_acc(rows):
    return (jnp.full((HEADS, rows), NEG, jnp.float32), jnp.zeros((HEADS, rows), jnp.float32), jnp.zeros((rows, HEADS, HEAD_DIM), jnp.float32))

def finish(acc):
    top, total, out = acc
    return (out / total.T[:, :, None]).astype(jnp.bfloat16)

def reference(video_query, video_value, audio_key, audio_value, video_proj, audio_proj, pair_first, pair_count):
    nblocks = N_SEQ
    vid_query = video_query.reshape(nblocks, VID_DEV, HEADS, HEAD_DIM)
    vid_value = video_value.reshape(nblocks, VID_DEV, HEADS, HEAD_DIM)
    aud_key = audio_key.reshape(nblocks, AUD_DEV, HEADS, HEAD_DIM)
    aud_value = audio_value.reshape(nblocks, AUD_DEV, HEADS, HEAD_DIM)

    def video_block(index):
        first = pair_first[index]
        count = pair_count[index]
        query = vid_query[index]
        acc = empty_acc(VID_DEV)
        for step in range(2 * HALF + 1):
            target = jnp.minimum(first + step, nblocks - 1).astype(jnp.int32)
            part = row_piece(tile_scores(query, aud_key[target]), aud_value[target])
            acc = combine(acc, masked(part, step < count))
        return finish(acc)

    def audio_block(index):
        keys = aud_key[index]
        acc = empty_acc(AUD_DEV)
        for offset in range(-HALF, HALF + 1):
            source = index + offset
            clipped = jnp.clip(source, 0, nblocks - 1).astype(jnp.int32)
            valid = (source >= 0) & (source < nblocks) & (pair_first[clipped] <= index) & (index < pair_first[clipped] + pair_count[clipped])
            part = col_piece(tile_scores(vid_query[clipped], keys), vid_value[clipped])
            acc = combine(acc, masked(part, valid))
        return finish(acc)
    blocks = jnp.arange(nblocks, dtype=jnp.int32)
    video_attn = lax.map(video_block, blocks).reshape(nblocks * VID_DEV, HEADS * HEAD_DIM)
    audio_attn = lax.map(audio_block, blocks).reshape(nblocks * AUD_DEV, HEADS * HEAD_DIM)
    video_out = jnp.dot(video_attn, video_proj, preferred_element_type=jnp.float32).astype(jnp.bfloat16)
    audio_out = jnp.dot(audio_attn, audio_proj, preferred_element_type=jnp.float32).astype(jnp.bfloat16)
    return (video_out, audio_out)
```

```python
import math

import jax
import jax.numpy as jnp
from jax import lax
from jax.experimental import pallas as pl
from jax.experimental.pallas import tpu as pltpu
from jax.sharding import PartitionSpec as P

HEAD_DIM = 128
HALF = 2


NEG = -1e30


def shifted(x, axis, by):
    size = lax.axis_size(axis)
    pairs = [(i, i + by) for i in range(size) if 0 <= i + by < size]
    return lax.ppermute(x, axis, pairs)


def tile_scores(query, keys):
    return jnp.einsum("vhe,ahe->hva", query, keys, preferred_element_type=jnp.float32) / math.sqrt(
        HEAD_DIM
    )


def row_piece(scores, values):
    top = jnp.max(scores, axis=2)
    expo = jnp.exp(scores - top[:, :, None])
    total = jnp.sum(expo, axis=2)
    out = jnp.einsum(
        "hva,ahe->vhe", expo.astype(jnp.bfloat16), values, preferred_element_type=jnp.float32
    )
    return (top, total, out)


def col_piece(scores, values):
    top = jnp.max(scores, axis=1)
    expo = jnp.exp(scores - top[:, None, :])
    total = jnp.sum(expo, axis=1)
    out = jnp.einsum(
        "hva,vhe->ahe", expo.astype(jnp.bfloat16), values, preferred_element_type=jnp.float32
    )
    return (top, total, out)


def combine(acc, part):
    top_a, total_a, out_a = acc
    top_b, total_b, out_b = part
    top = jnp.maximum(top_a, top_b)
    old = jnp.exp(top_a - top)
    new = jnp.exp(top_b - top)
    return (
        top,
        total_a * old + total_b * new,
        out_a * old.T[:, :, None] + out_b * new.T[:, :, None],
    )


def empty_acc(heads, rows):
    return (
        jnp.full((heads, rows), NEG, jnp.float32),
        jnp.zeros((heads, rows), jnp.float32),
        jnp.zeros((rows, heads, HEAD_DIM), jnp.float32),
    )


def finish(acc):
    top, total, out = acc
    result = (out / total.T[:, :, None]).astype(jnp.bfloat16)
    return result.reshape(result.shape[0], result.shape[1] * result.shape[2])


def safe_shards(
    video_query, video_value, audio_key, audio_value, video_proj, audio_proj, pair_first, pair_count
):
    heads = video_query.shape[1] // HEAD_DIM
    vid = video_query.shape[0]
    aud = audio_key.shape[0]
    nblocks = lax.axis_size("seq")
    me = lax.axis_index("seq")
    first = pair_first[me]
    count = pair_count[me]
    query = video_query.reshape(vid, heads, HEAD_DIM)
    own_keys = audio_key.reshape(aud, heads, HEAD_DIM)
    audio_pair = jnp.stack([audio_key, audio_value])
    video_pair = jnp.stack([video_query, video_value])
    video_acc = empty_acc(heads, vid)
    audio_acc = empty_acc(heads, aud)
    for offset in range(-HALF, HALF + 1):
        if offset == 0:
            arrived = audio_pair
        else:
            arrived = shifted(audio_pair, "seq", -offset)
        keys = arrived[0].reshape(aud, heads, HEAD_DIM)
        aud_vals = arrived[1].reshape(aud, heads, HEAD_DIM)
        target = me + offset
        valid = (target >= first) & (target < first + count)
        source = me - offset
        clipped = jnp.clip(source, 0, nblocks - 1)
        from_source = (
            (source >= 0)
            & (source < nblocks)
            & (pair_first[clipped] <= me)
            & (me < pair_first[clipped] + pair_count[clipped])
        )

        def video_side(unused):
            return row_piece(tile_scores(query, keys), aud_vals)

        def no_video(unused):
            return empty_acc(heads, vid)

        video_acc = combine(video_acc, lax.cond(valid, video_side, no_video, 0))
        if offset == 0:
            visiting = video_pair
        else:
            visiting = shifted(video_pair, "seq", offset)

        def audio_side(unused):
            visit_query = visiting[0].reshape(vid, heads, HEAD_DIM)
            visit_vals = visiting[1].reshape(vid, heads, HEAD_DIM)
            return col_piece(tile_scores(visit_query, own_keys), visit_vals)

        def no_audio(unused):
            return empty_acc(heads, aud)

        audio_acc = combine(audio_acc, lax.cond(from_source, audio_side, no_audio, 0))
    video_attn = finish(video_acc)
    audio_attn = finish(audio_acc)
    video_term = jnp.dot(video_attn, video_proj, preferred_element_type=jnp.float32)
    audio_term = jnp.dot(audio_attn, audio_proj, preferred_element_type=jnp.float32)
    video_sum, audio_sum = (
        lax.psum_scatter(video_term, "head", scatter_dimension=1, tiled=True),
        lax.psum_scatter(audio_term, "head", scatter_dimension=1, tiled=True),
    )
    return (video_sum.astype(jnp.bfloat16), audio_sum.astype(jnp.bfloat16))


GROUP = 4
SCALE = 1.4426950408889634 / math.sqrt(HEAD_DIM)
LOW, HIGH = 1e-25, 1e25


def pair_kernel(valid, x0, x1, x2, x3, prev, after, o_ref, u_ref, halo_ref, bad_ref, q, k, av, vv, o_acc, u_acc):
    vid = q.shape[1]
    aud = k.shape[1]
    av[:, :, HEAD_DIM:] = jnp.ones((2 * GROUP, aud, HEAD_DIM), jnp.bfloat16)
    vv[:, :, HEAD_DIM:] = jnp.ones((GROUP, vid, HEAD_DIM), jnp.bfloat16)
    for slot, x in enumerate((x0, x1, x2, x3)):
        q[slot] = x[:vid]
        vv[slot, :, :HEAD_DIM] = x[vid : 2 * vid]
        k[slot] = x[2 * vid : 2 * vid + aud]
        av[slot, :, :HEAD_DIM] = x[2 * vid + aud :]
    for slot, (x, at) in enumerate(((prev, 0), (prev, 1), (after, 0), (after, 1))):
        k[GROUP + slot] = x[at, :aud]
        av[GROUP + slot, :, :HEAD_DIM] = x[at, aud:]
    o_acc[...] = jnp.zeros_like(o_acc)
    u_acc[...] = jnp.zeros_like(u_acc)

    def step(pair, carry):
        row = pair // (2 * GROUP)
        col = pair % (2 * GROUP)

        @pl.when(valid[pair] != 0)
        def _():
            scores = lax.dot_general(
                q[row], k[col], (((1,), (1,)), ((), ())), preferred_element_type=jnp.float32
            )
            weights = jnp.exp2(scores * SCALE).astype(jnp.bfloat16)
            o_acc[row] += jnp.dot(weights, av[col], preferred_element_type=jnp.float32)
            u_acc[col] += lax.dot_general(
                weights, vv[row], (((0,), (0,)), ((), ())), preferred_element_type=jnp.float32
            )

        return carry

    lax.fori_loop(0, 2 * GROUP * GROUP, step, 0)
    bad = jnp.zeros((8, HEAD_DIM), jnp.float32)
    for slot in range(GROUP):
        total = o_acc[slot, :, HEAD_DIM:]
        o_ref[slot] = (o_acc[slot, :, :HEAD_DIM] / total).astype(jnp.bfloat16)
        wrong = jnp.where((total >= LOW) & (total <= HIGH), 0.0, 1.0)
        bad = jnp.maximum(bad, jnp.max(wrong.reshape(vid // 8, 8, HEAD_DIM), axis=0))
        u_ref[slot] = u_acc[slot]
        halo_ref[slot] = u_acc[GROUP + slot].astype(jnp.bfloat16)
    bad_ref[...] = bad


def pair_call(valid, parts, prev, after, vid, aud):
    vmem = pl.BlockSpec(memory_space=pltpu.VMEM)
    wide = 2 * HEAD_DIM
    tiles = 4 * GROUP
    return pl.pallas_call(
        pair_kernel,
        in_specs=[pl.BlockSpec(memory_space=pltpu.SMEM)] + [vmem] * 6,
        out_specs=[vmem] * 4,
        out_shape=[
            jax.ShapeDtypeStruct((GROUP, vid, HEAD_DIM), jnp.bfloat16),
            jax.ShapeDtypeStruct((GROUP, aud, wide), jnp.float32),
            jax.ShapeDtypeStruct((GROUP, aud, wide), jnp.bfloat16),
            jax.ShapeDtypeStruct((8, HEAD_DIM), jnp.float32),
        ],
        scratch_shapes=[
            pltpu.VMEM((GROUP, vid, HEAD_DIM), jnp.bfloat16),
            pltpu.VMEM((2 * GROUP, aud, HEAD_DIM), jnp.bfloat16),
            pltpu.VMEM((2 * GROUP, aud, wide), jnp.bfloat16),
            pltpu.VMEM((GROUP, vid, wide), jnp.bfloat16),
            pltpu.VMEM((GROUP, vid, wide), jnp.float32),
            pltpu.VMEM((2 * GROUP, aud, wide), jnp.float32),
        ],
        compiler_params=pltpu.CompilerParams(vmem_limit_bytes=48 * 1024 * 1024),
        cost_estimate=pl.CostEstimate(
            flops=tiles * 12 * vid * aud * HEAD_DIM,
            bytes_accessed=8 * 1024 * 1024,
            transcendentals=tiles * vid * aud,
        ),
    )(valid, *parts, prev, after)


def swap(x, distance):
    size = lax.axis_size("seq")
    return lax.ppermute(x, "seq", [(i, i ^ distance) for i in range(size)])


def pick(x, index):
    return lax.dynamic_index_in_dim(x, index, 0, keepdims=False)


def in_order(parts, place):
    odd = (place & 1) == 1
    parts = [jnp.where(odd, parts[d ^ 1], parts[d]) for d in range(GROUP)]
    high = (place & 2) == 2
    return [jnp.where(high, parts[d ^ 2], parts[d]) for d in range(GROUP)]


def fast_attention(video_query, video_value, audio_key, audio_value, pair_first, pair_count):
    vid, width = video_query.shape
    aud = audio_key.shape[0]
    heads = width // HEAD_DIM
    each = heads // GROUP
    me = lax.axis_index("seq")
    place = me % GROUP
    base = me - place
    slots = [place ^ d for d in range(GROUP)]
    video_blocks = jnp.stack([base + s for s in slots])
    audio_blocks = jnp.stack([base + s for s in slots] + [base - 2, base - 1, base + GROUP, base + GROUP + 1])
    first = pair_first[video_blocks][:, None]
    count = pair_count[video_blocks][:, None]
    valid = (audio_blocks[None, :] >= first) & (audio_blocks[None, :] < first + count)
    valid = valid.astype(jnp.int32).reshape(-1)

    video_pieces = [[] for _ in range(GROUP)]
    audio_pieces = [[] for _ in range(GROUP)]
    bads = []
    for t in range(each):
        parts = []
        for d in range(GROUP):
            column = (slots[d] * each + t) * HEAD_DIM
            piece = jnp.concatenate(
                [
                    lax.dynamic_slice_in_dim(x, column, HEAD_DIM, 1)
                    for x in (video_query, video_value, audio_key, audio_value)
                ]
            )
            parts.append(piece if d == 0 else swap(piece, d))
        keyed = in_order([x[2 * vid :] for x in parts], place)
        prev = shifted(jnp.stack(keyed[2:]), "seq", GROUP)
        after = shifted(jnp.stack(keyed[:2]), "seq", -GROUP)
        out, own, halo, bad = pair_call(valid, parts, prev, after, vid, aud)
        bads.append(jnp.max(bad))
        for d in range(GROUP):
            video_pieces[d].append(out[d] if d == 0 else swap(out[d], d))
        from_after = shifted(halo[:2], "seq", -GROUP)
        from_prev = shifted(halo[2:], "seq", GROUP)
        extra = jnp.concatenate([from_prev, from_after])
        for d in range(GROUP):
            both = own[d] + pick(extra, slots[d]).astype(jnp.float32)
            total = both[:, HEAD_DIM:]
            bads.append(jnp.max(jnp.where((total >= LOW) & (total <= HIGH), 0.0, 1.0)))
            piece = (both[:, :HEAD_DIM] / total).astype(jnp.bfloat16)
            audio_pieces[d].append(piece if d == 0 else swap(piece, d))
    video_attn = jnp.concatenate(
        in_order([jnp.concatenate(p, axis=1) for p in video_pieces], place), axis=1
    )
    audio_attn = jnp.concatenate(
        in_order([jnp.concatenate(p, axis=1) for p in audio_pieces], place), axis=1
    )
    return video_attn, audio_attn, jnp.max(jnp.stack(bads))


def shards(
    video_query, video_value, audio_key, audio_value, video_proj, audio_proj, pair_first, pair_count
):
    video_attn, audio_attn, bad = fast_attention(
        video_query, video_value, audio_key, audio_value, pair_first, pair_count
    )
    bad = lax.pmax(bad, ("seq", "head"))
    half = video_proj.shape[1] // 2
    core = lax.axis_index("head")

    def project(attn, proj):
        theirs = lax.dynamic_slice_in_dim(proj, (1 - core) * half, half, 1)
        mine = lax.dynamic_slice_in_dim(proj, core * half, half, 1)
        away = jnp.dot(attn, theirs, preferred_element_type=jnp.float32)
        arrived = lax.ppermute(away, "head", [(0, 1), (1, 0)])
        return (jnp.dot(attn, mine, preferred_element_type=jnp.float32) + arrived).astype(jnp.bfloat16)

    video_out = project(video_attn, video_proj)
    audio_out = project(audio_attn, audio_proj)
    return lax.cond(
        bad > 0,
        lambda args: safe_shards(*args),
        lambda args: (video_out, audio_out),
        (video_query, video_value, audio_key, audio_value, video_proj, audio_proj, pair_first, pair_count),
    )


def solution(mesh):
    in_specs = (
        P("seq", "head"),
        P("seq", "head"),
        P("seq", "head"),
        P("seq", "head"),
        P("head", None),
        P("head", None),
        P(),
        P(),
    )
    out_specs = (P("seq", "head"), P("seq", "head"))
    return jax.shard_map(shards, mesh=mesh, in_specs=in_specs, out_specs=out_specs, check_vma=False)
```

```python
import math

import jax
import jax.numpy as jnp
from jax import lax
from jax.experimental import pallas as pl
from jax.experimental.pallas import tpu as pltpu
from jax.sharding import PartitionSpec as P

HEAD_DIM = 128
GROUP = 4
NEG = -1e30
SCALE = 1.0 / math.sqrt(HEAD_DIM)
LOG2E = 1.4426950408889634
LOW, HIGH = 1e-25, 1e25
LOGICAL = pl.DeviceIdType.MESH


def greet(place, base, plane, planes):
    barrier = pltpu.get_barrier_semaphore()
    me = base + place
    for d in range(1, GROUP):
        pl.semaphore_signal(barrier, inc=1, device_id={"seq": base + (place ^ d)}, device_id_type=LOGICAL)

    @pl.when(plane > 0)
    def _():
        pl.semaphore_signal(barrier, inc=1, device_id={"seq": me - GROUP}, device_id_type=LOGICAL)

    @pl.when(plane < planes - 1)
    def _():
        pl.semaphore_signal(barrier, inc=1, device_id={"seq": me + GROUP}, device_id_type=LOGICAL)

    ends = jnp.minimum(plane, 1) + jnp.minimum(planes - 1 - plane, 1)
    pl.semaphore_wait(barrier, GROUP - 1 + ends)


def where_am_i(nblocks):
    me = lax.axis_index("seq")
    place = lax.rem(me, GROUP)
    return me, place, me - place, me // GROUP, nblocks // GROUP


def remote(src, dst, send, recv, target):
    return pltpu.make_async_remote_copy(
        src_ref=src, dst_ref=dst, send_sem=send, recv_sem=recv, device_id={"seq": target}, device_id_type=LOGICAL
    )


def gather_kernel(nblocks, width, k, av, q, vv, k_out, av_out, q_out, vv_out, send, recv, local, zsend, zrecv):
    me, place, base, plane, planes = where_am_i(nblocks)
    greet(place, base, plane, planes)
    pairs = ((k, k_out), (av, av_out), (q, q_out), (vv, vv_out))
    copies = {}
    for n, (src, dst) in enumerate(pairs):
        for d in (3, 1, 2):
            peer = place ^ d
            copies[n, d] = remote(
                src.at[:, pl.ds(pl.multiple_of(peer * width, width), width)],
                dst.at[place],
                send.at[n, d],
                recv.at[n, d],
                base + peer,
            )
            copies[n, d].start()
    own = []
    for n, (src, dst) in enumerate(pairs):
        copy = pltpu.make_async_copy(
            src.at[:, pl.ds(pl.multiple_of(place * width, width), width)], dst.at[place], local.at[n]
        )
        copy.start()
        own.append(copy)
    for n in range(2):
        own[n].wait()
        for d in range(1, GROUP):
            copies[n, d].wait_recv()
    up = [
        remote(x.at[pl.ds(2, 2)], x.at[pl.ds(GROUP, 2)], zsend.at[0, n], zrecv.at[0, n], me + GROUP)
        for n, x in enumerate((k_out, av_out))
    ]
    down = [
        remote(x.at[pl.ds(0, 2)], x.at[pl.ds(GROUP + 2, 2)], zsend.at[1, n], zrecv.at[1, n], me - GROUP)
        for n, x in enumerate((k_out, av_out))
    ]

    @pl.when(plane < planes - 1)
    def _():
        for copy in up:
            copy.start()

    @pl.when(plane > 0)
    def _():
        for copy in down:
            copy.start()

    for n in range(2, 4):
        own[n].wait()
        for d in range(1, GROUP):
            copies[n, d].wait_recv()
    for copy in copies.values():
        copy.wait_send()

    @pl.when(plane < planes - 1)
    def _():
        for copy in up:
            copy.wait_send()
        for copy in down:
            copy.wait_recv()

    @pl.when(plane > 0)
    def _():
        for copy in down:
            copy.wait_send()
        for copy in up:
            copy.wait_recv()


def gather(k, av, q, vv, nblocks):
    vid, aud = q.shape[0], k.shape[0]
    width = q.shape[1] // GROUP
    anyspace = pl.BlockSpec(memory_space=pl.ANY)
    return pl.pallas_call(
        lambda *refs: gather_kernel(nblocks, width, *refs),
        in_specs=[anyspace] * 4,
        out_specs=[anyspace] * 4,
        out_shape=[
            jax.ShapeDtypeStruct((2 * GROUP, aud, width), jnp.bfloat16),
            jax.ShapeDtypeStruct((2 * GROUP, aud, width), jnp.bfloat16),
            jax.ShapeDtypeStruct((GROUP, vid, width), jnp.bfloat16),
            jax.ShapeDtypeStruct((GROUP, vid, width), jnp.bfloat16),
        ],
        scratch_shapes=[
            pltpu.SemaphoreType.DMA((4, GROUP)),
            pltpu.SemaphoreType.DMA((4, GROUP)),
            pltpu.SemaphoreType.DMA((4,)),
            pltpu.SemaphoreType.DMA((2, 2)),
            pltpu.SemaphoreType.DMA((2, 2)),
        ],
        compiler_params=pltpu.CompilerParams(collective_id=0, has_side_effects=True),
    )(k, av, q, vv)


def pair_kernel(valid, k, av, q, vv, o_ref, u_ref, halo_ref, log_ref, avx, vvx, o_acc, u_acc, row_top, col_top):
    vid = q.shape[1]
    aud = k.shape[1]
    avx[:, :, :HEAD_DIM] = av[...]
    vvx[:, :, :HEAD_DIM] = vv[...]
    avx[:, :, HEAD_DIM:] = jnp.ones((2 * GROUP, aud, HEAD_DIM), jnp.bfloat16)
    vvx[:, :, HEAD_DIM:] = jnp.ones((GROUP, vid, HEAD_DIM), jnp.bfloat16)
    o_acc[...] = jnp.zeros_like(o_acc)
    u_acc[...] = jnp.zeros_like(u_acc)
    row_top[...] = jnp.zeros_like(row_top)
    col_top[...] = jnp.zeros_like(col_top)

    def each_pair(body):
        def step(pair, carry):
            @pl.when(valid[pair] != 0)
            def _():
                body(pair // (2 * GROUP), pair % (2 * GROUP))

            return carry

        lax.fori_loop(0, 2 * GROUP * GROUP, step, 0)

    def dot_t(a, b):
        return lax.dot_general(a, b, (((1,), (1,)), ((), ())), preferred_element_type=jnp.float32)

    def fast(row, col):
        weights = jnp.exp2(dot_t(q[row], k[col]) * (SCALE * LOG2E)).astype(jnp.bfloat16)
        o_acc[row] += jnp.dot(weights, avx[col], preferred_element_type=jnp.float32)
        u_acc[col] += lax.dot_general(
            weights, vvx[row], (((0,), (0,)), ((), ())), preferred_element_type=jnp.float32
        )

    each_pair(fast)

    def outside(total):
        wrong = jnp.where((total >= LOW) & (total <= HIGH), 0.0, 1.0)
        return jnp.max(wrong.reshape(-1, 8, HEAD_DIM), axis=0)

    bad = jnp.zeros((8, HEAD_DIM), jnp.float32)
    for slot in range(GROUP):
        bad = jnp.maximum(bad, outside(o_acc[slot, :, HEAD_DIM:]))
    for slot in range(2 * GROUP):
        used = valid[slot]
        for row in range(1, GROUP):
            used = jnp.maximum(used, valid[row * 2 * GROUP + slot])
        bad = jnp.maximum(bad, outside(u_acc[slot, :, HEAD_DIM:]) * used.astype(jnp.float32))

    @pl.when(jnp.max(bad) > 0)
    def _():
        o_acc[...] = jnp.zeros_like(o_acc)
        u_acc[...] = jnp.zeros_like(u_acc)
        row_top[...] = jnp.full_like(row_top, NEG)
        col_top[...] = jnp.full_like(col_top, NEG)

        def update(acc, top, at, scores, values):
            old = top[at]
            new = jnp.maximum(old, jnp.max(scores, axis=1, keepdims=True))
            weights = jnp.exp(scores - new[:, :1]).astype(jnp.bfloat16)
            shrink = jnp.exp(old[:, :1] - new[:, :1])
            top[at] = new
            acc[at] = acc[at] * shrink + jnp.dot(weights, values, preferred_element_type=jnp.float32)

        def safe(row, col):
            update(o_acc, row_top, row, dot_t(q[row], k[col]) * SCALE, avx[col])
            update(u_acc, col_top, col, dot_t(k[col], q[row]) * SCALE, vvx[row])

        each_pair(safe)

    for slot in range(GROUP):
        o_ref[slot] = (o_acc[slot, :, :HEAD_DIM] / o_acc[slot, :, HEAD_DIM:]).astype(jnp.bfloat16)
    for slot in range(2 * GROUP):
        total = u_acc[slot, :, HEAD_DIM:]
        some = total > 0
        mean = jnp.where(some, u_acc[slot, :, :HEAD_DIM] / jnp.where(some, total, 1.0), 0.0)
        logs = jnp.where(some, col_top[slot] + jnp.log(jnp.where(some, total, 1.0)), NEG)
        if slot < GROUP:
            u_ref[slot] = mean
        else:
            halo_ref[slot - GROUP] = mean.astype(jnp.bfloat16)
        log_ref[slot, 0] = jnp.transpose(logs)[:8]


def pair_call(valid, k, av, q, vv):
    vid, aud, width = q.shape[1], k.shape[1], q.shape[2]
    heads = width // HEAD_DIM
    wide = 2 * HEAD_DIM

    def block(*shape):
        return pl.BlockSpec(shape + (HEAD_DIM,), lambda h: (0, 0, h))

    return pl.pallas_call(
        pair_kernel,
        grid=(heads,),
        in_specs=[
            pl.BlockSpec(memory_space=pltpu.SMEM),
            block(2 * GROUP, aud),
            block(2 * GROUP, aud),
            block(GROUP, vid),
            block(GROUP, vid),
        ],
        out_specs=[
            block(GROUP, vid),
            block(GROUP, aud),
            block(GROUP, aud),
            pl.BlockSpec((2 * GROUP, 1, 8, aud), lambda h: (0, h, 0, 0)),
        ],
        out_shape=[
            jax.ShapeDtypeStruct((GROUP, vid, width), jnp.bfloat16),
            jax.ShapeDtypeStruct((GROUP, aud, width), jnp.float32),
            jax.ShapeDtypeStruct((GROUP, aud, width), jnp.bfloat16),
            jax.ShapeDtypeStruct((2 * GROUP, heads, 8, aud), jnp.float32),
        ],
        scratch_shapes=[
            pltpu.VMEM((2 * GROUP, aud, wide), jnp.bfloat16),
            pltpu.VMEM((GROUP, vid, wide), jnp.bfloat16),
            pltpu.VMEM((GROUP, vid, wide), jnp.float32),
            pltpu.VMEM((2 * GROUP, aud, wide), jnp.float32),
            pltpu.VMEM((GROUP, vid, HEAD_DIM), jnp.float32),
            pltpu.VMEM((2 * GROUP, aud, HEAD_DIM), jnp.float32),
        ],
        compiler_params=pltpu.CompilerParams(vmem_limit_bytes=48 * 1024 * 1024),
    )(valid, k, av, q, vv)


def back_kernel(
    nblocks, width, o, u, halo, logs, o_out, u_out, done, got, got_log, send, recv, local, zsend, zrecv
):
    me, place, base, plane, planes = where_am_i(nblocks)
    heads = width // HEAD_DIM
    greet(place, base, plane, planes)
    up = [
        remote(halo.at[pl.ds(2, 2)], got.at[pl.ds(0, 2)], zsend.at[0, 0], zrecv.at[0, 0], me + GROUP),
        remote(logs.at[pl.ds(GROUP + 2, 2)], got_log.at[pl.ds(0, 2)], zsend.at[0, 1], zrecv.at[0, 1], me + GROUP),
    ]
    down = [
        remote(halo.at[pl.ds(0, 2)], got.at[pl.ds(2, 2)], zsend.at[1, 0], zrecv.at[1, 0], me - GROUP),
        remote(logs.at[pl.ds(GROUP, 2)], got_log.at[pl.ds(2, 2)], zsend.at[1, 1], zrecv.at[1, 1], me - GROUP),
    ]

    @pl.when(plane < planes - 1)
    def _():
        for copy in up:
            copy.start()

    @pl.when(plane > 0)
    def _():
        for copy in down:
            copy.start()

    columns = pl.ds(pl.multiple_of(place * width, width), width)
    copies = {}
    for d in (3, 1, 2):
        peer = place ^ d
        copies[0, d] = remote(o.at[peer], o_out.at[:, columns], send.at[0, d], recv.at[0, d], base + peer)
        copies[0, d].start()
    own = pltpu.make_async_copy(o.at[place], o_out.at[:, columns], local.at[0])
    own.start()

    @pl.when(plane > 0)
    def _():
        for copy in up:
            copy.wait_recv()

    @pl.when(plane == 0)
    def _():
        got[0:2] = jnp.zeros((2,) + got.shape[1:], jnp.bfloat16)
        got_log[0:2] = jnp.full((2,) + got_log.shape[1:], NEG, jnp.float32)

    @pl.when(plane < planes - 1)
    def _():
        for copy in down:
            copy.wait_recv()

    @pl.when(plane == planes - 1)
    def _():
        got[2:4] = jnp.zeros((2,) + got.shape[1:], jnp.bfloat16)
        got_log[2:4] = jnp.full((2,) + got_log.shape[1:], NEG, jnp.float32)

    for slot in range(GROUP):
        for h in range(heads):
            cols = slice(h * HEAD_DIM, (h + 1) * HEAD_DIM)
            first, second = logs[slot, h], got_log[slot, h]
            top = jnp.maximum(first, second)
            a, b = jnp.exp(first - top), jnp.exp(second - top)
            share = a / (a + b)
            share = jnp.transpose(jnp.concatenate([share] * (HEAD_DIM // 8), axis=0))
            there = got[slot, :, cols].astype(jnp.float32)
            done[slot, :, cols] = (there + share * (u[slot, :, cols] - there)).astype(jnp.bfloat16)
    for d in (3, 1, 2):
        peer = place ^ d
        copies[1, d] = remote(done.at[peer], u_out.at[:, columns], send.at[1, d], recv.at[1, d], base + peer)
        copies[1, d].start()
    own_u = pltpu.make_async_copy(done.at[place], u_out.at[:, columns], local.at[1])
    own_u.start()
    own.wait()
    own_u.wait()
    for copy in copies.values():
        copy.wait()

    @pl.when(plane < planes - 1)
    def _():
        for copy in up:
            copy.wait_send()

    @pl.when(plane > 0)
    def _():
        for copy in down:
            copy.wait_send()


def give_back(o, u, halo, logs, nblocks):
    vid, aud, width = o.shape[1], u.shape[1], o.shape[2]
    anyspace = pl.BlockSpec(memory_space=pl.ANY)
    vmem = pl.BlockSpec(memory_space=pltpu.VMEM)
    return pl.pallas_call(
        lambda *refs: back_kernel(nblocks, width, *refs),
        in_specs=[anyspace, vmem, vmem, vmem],
        out_specs=[anyspace] * 2,
        out_shape=[
            jax.ShapeDtypeStruct((vid, GROUP * width), jnp.bfloat16),
            jax.ShapeDtypeStruct((aud, GROUP * width), jnp.bfloat16),
        ],
        scratch_shapes=[
            pltpu.VMEM((GROUP, aud, width), jnp.bfloat16),
            pltpu.VMEM((GROUP, aud, width), jnp.bfloat16),
            pltpu.VMEM((GROUP,) + logs.shape[1:], jnp.float32),
            pltpu.SemaphoreType.DMA((2, GROUP)),
            pltpu.SemaphoreType.DMA((2, GROUP)),
            pltpu.SemaphoreType.DMA((2,)),
            pltpu.SemaphoreType.DMA((2, 2)),
            pltpu.SemaphoreType.DMA((2, 2)),
        ],
        compiler_params=pltpu.CompilerParams(
            collective_id=1, has_side_effects=True, vmem_limit_bytes=48 * 1024 * 1024
        ),
    )(o, u, halo, logs)


def shards(
    video_query, video_value, audio_key, audio_value, video_proj, audio_proj, pair_first, pair_count
):
    nblocks = lax.axis_size("seq")
    me = lax.axis_index("seq")
    base = me - me % GROUP
    audio_blocks = base + jnp.asarray(list(range(GROUP)) + [-2, -1, GROUP, GROUP + 1])
    first = lax.dynamic_slice_in_dim(pair_first, base, GROUP)[:, None]
    count = lax.dynamic_slice_in_dim(pair_count, base, GROUP)[:, None]
    valid = (audio_blocks[None, :] >= first) & (audio_blocks[None, :] < first + count)
    valid = valid.astype(jnp.int32).reshape(-1)
    k, av, q, vv = gather(audio_key, audio_value, video_query, video_value, nblocks)
    o, u, halo, logs = pair_call(valid, k, av, q, vv)
    video_attn, audio_attn = give_back(o, u, halo, logs, nblocks)
    half = video_proj.shape[1] // 2
    core = lax.axis_index("head")
    attns = (video_attn, audio_attn)
    projs = (video_proj, audio_proj)

    def part(attn, proj, which):
        columns = lax.dynamic_slice_in_dim(proj, which * half, half, 1)
        return jnp.dot(attn, columns, preferred_element_type=jnp.float32)

    away = [part(a, p, 1 - core) for a, p in zip(attns, projs)]
    arrived = [lax.ppermute(x, "head", [(0, 1), (1, 0)]) for x in away]
    return tuple((part(a, p, core) + x).astype(jnp.bfloat16) for a, p, x in zip(attns, projs, arrived))


def solution(mesh):
    in_specs = (
        P("seq", "head"),
        P("seq", "head"),
        P("seq", "head"),
        P("seq", "head"),
        P("head", None),
        P("head", None),
        P(),
        P(),
    )
    out_specs = (P("seq", "head"), P("seq", "head"))
    return jax.shard_map(shards, mesh=mesh, in_specs=in_specs, out_specs=out_specs, check_vma=False)
```

```python
import math

import jax
import jax.numpy as jnp
from jax import lax
from jax.experimental import pallas as pl
from jax.experimental.pallas import tpu as pltpu
from jax.sharding import PartitionSpec as P

HEAD_DIM = 128
GROUP = 4
HALF = 2
NEG = -1e30
SCALE = 1.0 / math.sqrt(HEAD_DIM)
LOG2E = 1.4426950408889634
LOW, HIGH = 1e-25, 1e25
LOGICAL = pl.DeviceIdType.MESH


def greet(place, base, plane, planes):
    barrier = pltpu.get_barrier_semaphore()
    me = base + place
    for d in range(1, GROUP):
        pl.semaphore_signal(barrier, inc=1, device_id={"seq": base + (place ^ d)}, device_id_type=LOGICAL)

    @pl.when(plane > 0)
    def _():
        pl.semaphore_signal(barrier, inc=1, device_id={"seq": me - GROUP}, device_id_type=LOGICAL)

    @pl.when(plane < planes - 1)
    def _():
        pl.semaphore_signal(barrier, inc=1, device_id={"seq": me + GROUP}, device_id_type=LOGICAL)

    ends = jnp.minimum(plane, 1) + jnp.minimum(planes - 1 - plane, 1)
    pl.semaphore_wait(barrier, GROUP - 1 + ends)


def where_am_i(nblocks):
    me = lax.axis_index("seq")
    place = lax.rem(me, GROUP)
    return me, place, me - place, me // GROUP, nblocks // GROUP


def remote(src, dst, send, recv, target):
    return pltpu.make_async_remote_copy(
        src_ref=src, dst_ref=dst, send_sem=send, recv_sem=recv, device_id={"seq": target}, device_id_type=LOGICAL
    )


SPAN = 2 * HALF + 1
SLOTS = GROUP + 2 * HALF
OWN = (4, 5, 0, 1, 2, 3, 6, 7)


def dot_t(a, b):
    return lax.dot_general(a, b, (((1,), (1,)), ((), ())), preferred_element_type=jnp.float32)


def write_audio(t, slot, total, summed, top, u_ref, halo_ref, log_ref):
    some = total > 0
    mean = jnp.where(some, summed / jnp.where(some, total, 1.0), 0.0)
    logs = jnp.where(some, top + jnp.log(jnp.where(some, total, 1.0)), NEG)
    place = OWN[slot]
    columns = slice(t * HEAD_DIM, (t + 1) * HEAD_DIM)
    if place < GROUP:
        u_ref[place, :, columns] = mean
    else:
        halo_ref[place - GROUP, :, columns] = mean.astype(jnp.bfloat16)
    log_ref[place, t] = jnp.transpose(logs)[:8]


def pair_kernel(
    nblocks, heads, bias, used, k, av, q, vv,
    k_buf, av_buf, q_buf, vv_buf, o_ref, u_ref, halo_ref, log_ref, bad_ref,
    avx, vvx, u_acc, send, recv, local, zsend, zrecv,
):
    me, place, base, plane, planes = where_am_i(nblocks)
    vid, aud = q.shape[0], k.shape[0]
    greet(place, base, plane, planes)
    arrays = ((k, k_buf, HALF), (av, av_buf, HALF), (q, q_buf, 0), (vv, vv_buf, 0))

    def column(member, t):
        return pl.ds(pl.multiple_of((member * heads + t) * HEAD_DIM, HEAD_DIM), HEAD_DIM)

    copies, own = {}, {}
    for t in range(heads):
        for n, (src, dst, at) in enumerate(arrays):
            for d in (3, 1, 2):
                peer = place ^ d
                copies[t, n, d] = remote(
                    src.at[:, column(peer, t)], dst.at[t, place + at], send.at[t, n, d], recv.at[t, n, d], base + peer
                )
                copies[t, n, d].start()
    for t in range(heads):
        for n, (src, dst, at) in enumerate(arrays):
            own[t, n] = pltpu.make_async_copy(src.at[:, column(place, t)], dst.at[t, place + at], local.at[t, n])
            own[t, n].start()

    def relays(t, up):
        source, target = (GROUP, 0) if up else (HALF, GROUP + HALF)
        side = 0 if up else 1
        return [
            remote(
                x.at[t, pl.ds(source, HALF)],
                x.at[t, pl.ds(target, HALF)],
                zsend.at[t, side, n],
                zrecv.at[t, side, n],
                me + GROUP if up else me - GROUP,
            )
            for n, x in enumerate((k_buf, av_buf))
        ]

    avx[:, :, HEAD_DIM:] = jnp.ones((SLOTS, aud, HEAD_DIM), jnp.bfloat16)
    vvx[:, :, HEAD_DIM:] = jnp.ones((GROUP, vid, HEAD_DIM), jnp.bfloat16)

    @pl.when(plane == 0)
    def _():
        for x in (k_buf, av_buf):
            x[:, :HALF] = jnp.zeros((heads, HALF, aud, HEAD_DIM), jnp.bfloat16)

    @pl.when(plane == planes - 1)
    def _():
        for x in (k_buf, av_buf):
            x[:, GROUP + HALF :] = jnp.zeros((heads, HALF, aud, HEAD_DIM), jnp.bfloat16)

    def outside(total):
        wrong = jnp.where((total >= LOW) & (total <= HIGH), 0.0, 1.0)
        return jnp.max(wrong.reshape(-1, 8, HEAD_DIM), axis=0)

    bad_ref[...] = jnp.zeros_like(bad_ref)
    for t in range(heads):
        for n in range(4):
            own[t, n].wait()
            for d in range(1, GROUP):
                copies[t, n, d].wait_recv()
            if n == 1:

                @pl.when(plane < planes - 1)
                def _():
                    for copy in relays(t, True):
                        copy.start()

                @pl.when(plane > 0)
                def _():
                    for copy in relays(t, False):
                        copy.start()

        @pl.when(plane < planes - 1)
        def _():
            for copy in relays(t, False):
                copy.wait_recv()

        @pl.when(plane > 0)
        def _():
            for copy in relays(t, True):
                copy.wait_recv()

        avx[:, :, :HEAD_DIM] = av_buf[t]
        vvx[:, :, :HEAD_DIM] = vv_buf[t]
        u_acc[...] = jnp.zeros_like(u_acc)
        columns = slice(t * HEAD_DIM, (t + 1) * HEAD_DIM)

        def step(row, carry):
            query = q_buf[t, row]
            weights = jnp.concatenate(
                [
                    jnp.exp2(
                        dot_t(query, k_buf[t, row + c]) * (SCALE * LOG2E) + bias[row * SPAN + c]
                    ).astype(jnp.bfloat16)
                    for c in range(SPAN)
                ],
                axis=1,
            )
            values = avx[pl.ds(row, SPAN)].reshape(SPAN * aud, 2 * HEAD_DIM)
            out = jnp.dot(weights, values, preferred_element_type=jnp.float32)
            total = out[:, HEAD_DIM:]
            o_ref[row, :, columns] = (out[:, :HEAD_DIM] / total).astype(jnp.bfloat16)
            bad_ref[...] = jnp.maximum(bad_ref[...], outside(total))
            back = lax.dot_general(
                weights, vvx[row], (((0,), (0,)), ((), ())), preferred_element_type=jnp.float32
            )
            u_acc[pl.ds(row, SPAN)] += back.reshape(SPAN, aud, 2 * HEAD_DIM)
            return carry

        lax.fori_loop(0, GROUP, step, 0)
        for slot in range(SLOTS):
            total = u_acc[slot, :, HEAD_DIM:]
            bad_ref[...] = jnp.maximum(bad_ref[...], outside(total) * used[slot])
            write_audio(t, slot, total, u_acc[slot, :, :HEAD_DIM], 0.0, u_ref, halo_ref, log_ref)

    for copy in copies.values():
        copy.wait_send()

    @pl.when(plane < planes - 1)
    def _():
        for t in range(heads):
            for copy in relays(t, True):
                copy.wait_send()

    @pl.when(plane > 0)
    def _():
        for t in range(heads):
            for copy in relays(t, False):
                copy.wait_send()


def result_shapes(vid, aud, heads):
    width = heads * HEAD_DIM
    return [
        jax.ShapeDtypeStruct((GROUP, vid, width), jnp.bfloat16),
        jax.ShapeDtypeStruct((GROUP, aud, width), jnp.float32),
        jax.ShapeDtypeStruct((GROUP, aud, width), jnp.bfloat16),
        jax.ShapeDtypeStruct((SLOTS, heads, 8, aud), jnp.float32),
    ]


def pair_call(bias, used, k, av, q, vv, nblocks):
    vid, aud = q.shape[0], k.shape[0]
    heads = q.shape[1] // HEAD_DIM // GROUP
    wide = 2 * HEAD_DIM
    anyspace = pl.BlockSpec(memory_space=pl.ANY)
    smem = pl.BlockSpec(memory_space=pltpu.SMEM)
    vmem = pl.BlockSpec(memory_space=pltpu.VMEM)
    audio = jax.ShapeDtypeStruct((heads, SLOTS, aud, HEAD_DIM), jnp.bfloat16)
    video = jax.ShapeDtypeStruct((heads, GROUP, vid, HEAD_DIM), jnp.bfloat16)
    return pl.pallas_call(
        lambda *refs: pair_kernel(nblocks, heads, *refs),
        in_specs=[smem, smem] + [anyspace] * 4,
        out_specs=[vmem] * 9,
        out_shape=[audio, audio, video, video]
        + result_shapes(vid, aud, heads)
        + [jax.ShapeDtypeStruct((8, HEAD_DIM), jnp.float32)],
        scratch_shapes=[
            pltpu.VMEM((SLOTS, aud, wide), jnp.bfloat16),
            pltpu.VMEM((GROUP, vid, wide), jnp.bfloat16),
            pltpu.VMEM((SLOTS, aud, wide), jnp.float32),
            pltpu.SemaphoreType.DMA((heads, 4, GROUP)),
            pltpu.SemaphoreType.DMA((heads, 4, GROUP)),
            pltpu.SemaphoreType.DMA((heads, 4)),
            pltpu.SemaphoreType.DMA((heads, 2, 2)),
            pltpu.SemaphoreType.DMA((heads, 2, 2)),
        ],
        compiler_params=pltpu.CompilerParams(
            collective_id=0, has_side_effects=True, vmem_limit_bytes=50 * 1024 * 1024
        ),
    )(bias, used, k, av, q, vv)


def safe_kernel(heads, bias, k, av, q, vv, o_ref, u_ref, halo_ref, log_ref, o_acc, u_acc, row_top, col_top):
    wide = o_acc.shape[-1]
    for t in range(heads):
        o_acc[...] = jnp.zeros_like(o_acc)
        u_acc[...] = jnp.zeros_like(u_acc)
        row_top[...] = jnp.full_like(row_top, NEG)
        col_top[...] = jnp.full_like(col_top, NEG)

        def update(acc, top, at, scores, values):
            old = top[at]
            new = jnp.maximum(old, jnp.max(scores, axis=1, keepdims=True))
            weights = jnp.exp(scores - new[:, :1]).astype(jnp.bfloat16)
            values = jnp.concatenate([values, jnp.ones_like(values)], axis=1)
            top[at] = new
            acc[at] = acc[at] * jnp.exp(old[:, :1] - new[:, :1]) + jnp.dot(
                weights, values, preferred_element_type=jnp.float32
            )

        def step(pair, carry):
            row = pair // SPAN
            col = row + pair % SPAN

            @pl.when(bias[pair] > -1.0)
            def _():
                query, keys = q[t, row], k[t, col]
                update(o_acc, row_top, row, dot_t(query, keys) * SCALE, av[t, col])
                update(u_acc, col_top, col, dot_t(keys, query) * SCALE, vv[t, row])

            return carry

        lax.fori_loop(0, GROUP * SPAN, step, 0)
        columns = slice(t * HEAD_DIM, (t + 1) * HEAD_DIM)
        for row in range(GROUP):
            o_ref[row, :, columns] = (o_acc[row, :, :HEAD_DIM] / o_acc[row, :, HEAD_DIM:]).astype(jnp.bfloat16)
        for slot in range(SLOTS):
            write_audio(
                t, slot, u_acc[slot, :, HEAD_DIM:], u_acc[slot, :, :HEAD_DIM], col_top[slot], u_ref, halo_ref, log_ref
            )


def safe_call(bias, k, av, q, vv):
    heads, _, vid, _ = q.shape
    aud = k.shape[2]
    wide = 2 * HEAD_DIM
    vmem = pl.BlockSpec(memory_space=pltpu.VMEM)
    return pl.pallas_call(
        lambda *refs: safe_kernel(heads, *refs),
        in_specs=[pl.BlockSpec(memory_space=pltpu.SMEM)] + [vmem] * 4,
        out_specs=[vmem] * 4,
        out_shape=result_shapes(vid, aud, heads),
        scratch_shapes=[
            pltpu.VMEM((GROUP, vid, wide), jnp.float32),
            pltpu.VMEM((SLOTS, aud, wide), jnp.float32),
            pltpu.VMEM((GROUP, vid, HEAD_DIM), jnp.float32),
            pltpu.VMEM((SLOTS, aud, HEAD_DIM), jnp.float32),
        ],
        compiler_params=pltpu.CompilerParams(vmem_limit_bytes=50 * 1024 * 1024),
    )(bias, k, av, q, vv)


def back_kernel(
    nblocks, width, o, u, halo, logs, o_out, u_out, done, got, got_log, send, recv, local, zsend, zrecv
):
    me, place, base, plane, planes = where_am_i(nblocks)
    heads = width // HEAD_DIM
    greet(place, base, plane, planes)
    up = [
        remote(halo.at[pl.ds(2, 2)], got.at[pl.ds(0, 2)], zsend.at[0, 0], zrecv.at[0, 0], me + GROUP),
        remote(logs.at[pl.ds(GROUP + 2, 2)], got_log.at[pl.ds(0, 2)], zsend.at[0, 1], zrecv.at[0, 1], me + GROUP),
    ]
    down = [
        remote(halo.at[pl.ds(0, 2)], got.at[pl.ds(2, 2)], zsend.at[1, 0], zrecv.at[1, 0], me - GROUP),
        remote(logs.at[pl.ds(GROUP, 2)], got_log.at[pl.ds(2, 2)], zsend.at[1, 1], zrecv.at[1, 1], me - GROUP),
    ]

    @pl.when(plane < planes - 1)
    def _():
        for copy in up:
            copy.start()

    @pl.when(plane > 0)
    def _():
        for copy in down:
            copy.start()

    columns = pl.ds(pl.multiple_of(place * width, width), width)
    copies = {}
    for d in (3, 1, 2):
        peer = place ^ d
        copies[0, d] = remote(o.at[peer], o_out.at[:, columns], send.at[0, d], recv.at[0, d], base + peer)
        copies[0, d].start()
    own = pltpu.make_async_copy(o.at[place], o_out.at[:, columns], local.at[0])
    own.start()

    @pl.when(plane > 0)
    def _():
        for copy in up:
            copy.wait_recv()

    @pl.when(plane == 0)
    def _():
        got[0:2] = jnp.zeros((2,) + got.shape[1:], jnp.bfloat16)
        got_log[0:2] = jnp.full((2,) + got_log.shape[1:], NEG, jnp.float32)

    @pl.when(plane < planes - 1)
    def _():
        for copy in down:
            copy.wait_recv()

    @pl.when(plane == planes - 1)
    def _():
        got[2:4] = jnp.zeros((2,) + got.shape[1:], jnp.bfloat16)
        got_log[2:4] = jnp.full((2,) + got_log.shape[1:], NEG, jnp.float32)

    for slot in range(GROUP):
        for h in range(heads):
            cols = slice(h * HEAD_DIM, (h + 1) * HEAD_DIM)
            first, second = logs[slot, h], got_log[slot, h]
            top = jnp.maximum(first, second)
            a, b = jnp.exp(first - top), jnp.exp(second - top)
            share = a / (a + b)
            share = jnp.transpose(jnp.concatenate([share] * (HEAD_DIM // 8), axis=0))
            there = got[slot, :, cols].astype(jnp.float32)
            done[slot, :, cols] = (there + share * (u[slot, :, cols] - there)).astype(jnp.bfloat16)
    for d in (3, 1, 2):
        peer = place ^ d
        copies[1, d] = remote(done.at[peer], u_out.at[:, columns], send.at[1, d], recv.at[1, d], base + peer)
        copies[1, d].start()
    own_u = pltpu.make_async_copy(done.at[place], u_out.at[:, columns], local.at[1])
    own_u.start()
    own.wait()
    own_u.wait()
    for copy in copies.values():
        copy.wait()

    @pl.when(plane < planes - 1)
    def _():
        for copy in up:
            copy.wait_send()

    @pl.when(plane > 0)
    def _():
        for copy in down:
            copy.wait_send()


def give_back(o, u, halo, logs, nblocks):
    vid, aud, width = o.shape[1], u.shape[1], o.shape[2]
    anyspace = pl.BlockSpec(memory_space=pl.ANY)
    vmem = pl.BlockSpec(memory_space=pltpu.VMEM)
    return pl.pallas_call(
        lambda *refs: back_kernel(nblocks, width, *refs),
        in_specs=[anyspace, vmem, vmem, vmem],
        out_specs=[anyspace] * 2,
        out_shape=[
            jax.ShapeDtypeStruct((vid, GROUP * width), jnp.bfloat16),
            jax.ShapeDtypeStruct((aud, GROUP * width), jnp.bfloat16),
        ],
        scratch_shapes=[
            pltpu.VMEM((GROUP, aud, width), jnp.bfloat16),
            pltpu.VMEM((GROUP, aud, width), jnp.bfloat16),
            pltpu.VMEM((GROUP,) + logs.shape[1:], jnp.float32),
            pltpu.SemaphoreType.DMA((2, GROUP)),
            pltpu.SemaphoreType.DMA((2, GROUP)),
            pltpu.SemaphoreType.DMA((2,)),
            pltpu.SemaphoreType.DMA((2, 2)),
            pltpu.SemaphoreType.DMA((2, 2)),
        ],
        compiler_params=pltpu.CompilerParams(
            collective_id=1, has_side_effects=True, vmem_limit_bytes=48 * 1024 * 1024
        ),
    )(o, u, halo, logs)


def shards(
    video_query, video_value, audio_key, audio_value, video_proj, audio_proj, pair_first, pair_count
):
    nblocks = lax.axis_size("seq")
    me = lax.axis_index("seq")
    base = me - me % GROUP
    offsets = jnp.arange(SPAN)[None, :] - HALF + base + jnp.arange(GROUP)[:, None]
    first = lax.dynamic_slice_in_dim(pair_first, base, GROUP)[:, None]
    count = lax.dynamic_slice_in_dim(pair_count, base, GROUP)[:, None]
    valid = (offsets >= first) & (offsets < first + count)
    bias = jnp.where(valid, 0.0, NEG).astype(jnp.float32).reshape(-1)
    hits = [[valid[r, c] for r in range(GROUP) for c in range(SPAN) if r + c == s] for s in range(SLOTS)]
    used = jnp.stack([jnp.any(jnp.stack(x)) for x in hits]).astype(jnp.float32)
    *held, o, u, halo, logs, bad = pair_call(
        bias, used, audio_key, audio_value, video_query, video_value, nblocks
    )
    o, u, halo, logs = lax.cond(
        jnp.max(bad) > 0, lambda: tuple(safe_call(bias, *held)), lambda: (o, u, halo, logs)
    )
    video_attn, audio_attn = give_back(o, u, halo, logs, nblocks)
    half = video_proj.shape[1] // 2
    core = lax.axis_index("head")
    attns = (video_attn, audio_attn)
    projs = (video_proj, audio_proj)

    def part(attn, proj, which):
        columns = lax.dynamic_slice_in_dim(proj, which * half, half, 1)
        return jnp.dot(attn, columns, preferred_element_type=jnp.float32)

    away = [part(a, p, 1 - core) for a, p in zip(attns, projs)]
    arrived = [lax.ppermute(x, "head", [(0, 1), (1, 0)]) for x in away]
    return tuple((part(a, p, core) + x).astype(jnp.bfloat16) for a, p, x in zip(attns, projs, arrived))


def solution(mesh):
    in_specs = (
        P("seq", "head"),
        P("seq", "head"),
        P("seq", "head"),
        P("seq", "head"),
        P("head", None),
        P("head", None),
        P(),
        P(),
    )
    out_specs = (P("seq", "head"), P("seq", "head"))
    return jax.shard_map(shards, mesh=mesh, in_specs=in_specs, out_specs=out_specs, check_vma=False)
```

```python
import math

import jax
import jax.numpy as jnp
from jax import lax
from jax.experimental import pallas as pl
from jax.experimental.pallas import tpu as pltpu
from jax.sharding import PartitionSpec as P

HEAD_DIM = 128
GROUP = 4
HALF = 2
NEG = -1e30
SCALE = 1.0 / math.sqrt(HEAD_DIM)
LOG2E = 1.4426950408889634
LOW, HIGH = 1e-25, 1e25
LOGICAL = pl.DeviceIdType.MESH


def greet(place, base, plane, planes, other=None):
    barrier = pltpu.get_barrier_semaphore()
    me = base + place
    for d in range(1, GROUP):
        pl.semaphore_signal(barrier, inc=1, device_id={"seq": base + (place ^ d)}, device_id_type=LOGICAL)

    @pl.when(plane > 0)
    def _():
        pl.semaphore_signal(barrier, inc=1, device_id={"seq": me - GROUP}, device_id_type=LOGICAL)

    @pl.when(plane < planes - 1)
    def _():
        pl.semaphore_signal(barrier, inc=1, device_id={"seq": me + GROUP}, device_id_type=LOGICAL)

    if other is not None:
        pl.semaphore_signal(barrier, inc=1, device_id={"head": other}, device_id_type=LOGICAL)
    ends = (0 if other is None else 1) + jnp.minimum(plane, 1) + jnp.minimum(planes - 1 - plane, 1)
    pl.semaphore_wait(barrier, GROUP - 1 + ends)


def where_am_i(nblocks):
    me = lax.axis_index("seq")
    place = lax.rem(me, GROUP)
    return me, place, me - place, me // GROUP, nblocks // GROUP


def remote(src, dst, send, recv, target):
    return pltpu.make_async_remote_copy(
        src_ref=src, dst_ref=dst, send_sem=send, recv_sem=recv, device_id={"seq": target}, device_id_type=LOGICAL
    )


TILE = 512
SPAN = 2 * HALF + 1
SLOTS = GROUP + 2 * HALF
OWN = (4, 5, 0, 1, 2, 3, 6, 7)


def dot_t(a, b):
    return lax.dot_general(a, b, (((1,), (1,)), ((), ())), preferred_element_type=jnp.float32)


def write_audio(t, slot, total, summed, top, u_ref, halo_ref, log_ref):
    some = total > 0
    mean = jnp.where(some, summed / jnp.where(some, total, 1.0), 0.0)
    logs = jnp.where(some, top + jnp.log(jnp.where(some, total, 1.0)), NEG)
    place = OWN[slot]
    columns = slice(t * HEAD_DIM, (t + 1) * HEAD_DIM)
    if place < GROUP:
        u_ref[place, :, columns] = mean
    else:
        halo_ref[place - GROUP, :, columns] = mean.astype(jnp.bfloat16)
    log_ref[place, t] = jnp.transpose(logs)[:8]


def pair_kernel(
    nblocks, heads, bias, used, k, av, q, vv,
    k_buf, av_buf, q_buf, vv_buf, o_ref, u_ref, halo_ref, log_ref, bad_ref,
    avx, vvx, u_acc, send, recv, local, zsend, zrecv,
):
    me, place, base, plane, planes = where_am_i(nblocks)
    vid, aud = q.shape[0], k.shape[0]
    greet(place, base, plane, planes)
    arrays = ((k, k_buf, HALF), (av, av_buf, HALF), (q, q_buf, 0), (vv, vv_buf, 0))

    def column(member, t):
        return pl.ds(pl.multiple_of((member * heads + t) * HEAD_DIM, HEAD_DIM), HEAD_DIM)

    copies, own = {}, {}
    for t in range(heads):
        for n, (src, dst, at) in enumerate(arrays):
            for d in (3, 1, 2):
                peer = place ^ d
                copies[t, n, d] = remote(
                    src.at[:, column(peer, t)], dst.at[t, place + at], send.at[t, n, d], recv.at[t, n, d], base + peer
                )
                copies[t, n, d].start()
    for t in range(heads):
        for n, (src, dst, at) in enumerate(arrays):
            own[t, n] = pltpu.make_async_copy(src.at[:, column(place, t)], dst.at[t, place + at], local.at[t, n])
            own[t, n].start()

    def relays(t, up):
        source, target = (GROUP, 0) if up else (HALF, GROUP + HALF)
        side = 0 if up else 1
        return [
            remote(
                x.at[t, pl.ds(source, HALF)],
                x.at[t, pl.ds(target, HALF)],
                zsend.at[t, side, n],
                zrecv.at[t, side, n],
                me + GROUP if up else me - GROUP,
            )
            for n, x in enumerate((k_buf, av_buf))
        ]

    avx[:, :, HEAD_DIM:] = jnp.ones((SLOTS, aud, HEAD_DIM), jnp.bfloat16)
    vvx[:, :, HEAD_DIM:] = jnp.ones((GROUP, vid, HEAD_DIM), jnp.bfloat16)

    @pl.when(plane == 0)
    def _():
        for x in (k_buf, av_buf):
            x[:, :HALF] = jnp.zeros((heads, HALF, aud, HEAD_DIM), jnp.bfloat16)

    @pl.when(plane == planes - 1)
    def _():
        for x in (k_buf, av_buf):
            x[:, GROUP + HALF :] = jnp.zeros((heads, HALF, aud, HEAD_DIM), jnp.bfloat16)

    def outside(total):
        wrong = jnp.where((total >= LOW) & (total <= HIGH), 0.0, 1.0)
        return jnp.max(wrong.reshape(-1, 8, HEAD_DIM), axis=0)

    bad_ref[...] = jnp.zeros_like(bad_ref)
    for t in range(heads):
        for n in range(4):
            own[t, n].wait()
            for d in range(1, GROUP):
                copies[t, n, d].wait_recv()
            if n == 1:

                @pl.when(plane < planes - 1)
                def _():
                    for copy in relays(t, True):
                        copy.start()

                @pl.when(plane > 0)
                def _():
                    for copy in relays(t, False):
                        copy.start()

        @pl.when(plane < planes - 1)
        def _():
            for copy in relays(t, False):
                copy.wait_recv()

        @pl.when(plane > 0)
        def _():
            for copy in relays(t, True):
                copy.wait_recv()

        avx[:, :, :HEAD_DIM] = av_buf[t]
        vvx[:, :, :HEAD_DIM] = vv_buf[t]
        u_acc[...] = jnp.zeros_like(u_acc)
        columns = slice(t * HEAD_DIM, (t + 1) * HEAD_DIM)

        def step(row, carry):
            query = q_buf[t, row]
            weights = jnp.concatenate(
                [
                    jnp.exp2(
                        dot_t(query, k_buf[t, row + c]) * (SCALE * LOG2E) + bias[row * SPAN + c]
                    ).astype(jnp.bfloat16)
                    for c in range(SPAN)
                ],
                axis=1,
            )
            values = avx[pl.ds(row, SPAN)].reshape(SPAN * aud, 2 * HEAD_DIM)
            out = jnp.dot(weights, values, preferred_element_type=jnp.float32)
            total = out[:, HEAD_DIM:]
            o_ref[row, :, columns] = (out[:, :HEAD_DIM] / total).astype(jnp.bfloat16)
            bad_ref[...] = jnp.maximum(bad_ref[...], outside(total))
            back = lax.dot_general(
                weights, vvx[row], (((0,), (0,)), ((), ())), preferred_element_type=jnp.float32
            )
            u_acc[pl.ds(row, SPAN)] += back.reshape(SPAN, aud, 2 * HEAD_DIM)
            return carry

        lax.fori_loop(0, GROUP, step, 0)
        for slot in range(SLOTS):
            total = u_acc[slot, :, HEAD_DIM:]
            bad_ref[...] = jnp.maximum(bad_ref[...], outside(total) * used[slot])
            write_audio(t, slot, total, u_acc[slot, :, :HEAD_DIM], 0.0, u_ref, halo_ref, log_ref)

    for copy in copies.values():
        copy.wait_send()

    @pl.when(plane < planes - 1)
    def _():
        for t in range(heads):
            for copy in relays(t, True):
                copy.wait_send()

    @pl.when(plane > 0)
    def _():
        for t in range(heads):
            for copy in relays(t, False):
                copy.wait_send()


def result_shapes(vid, aud, heads):
    width = heads * HEAD_DIM
    return [
        jax.ShapeDtypeStruct((GROUP, vid, width), jnp.bfloat16),
        jax.ShapeDtypeStruct((GROUP, aud, width), jnp.float32),
        jax.ShapeDtypeStruct((GROUP, aud, width), jnp.bfloat16),
        jax.ShapeDtypeStruct((SLOTS, heads, 8, aud), jnp.float32),
    ]


def pair_call(bias, used, k, av, q, vv, nblocks):
    vid, aud = q.shape[0], k.shape[0]
    heads = q.shape[1] // HEAD_DIM // GROUP
    wide = 2 * HEAD_DIM
    anyspace = pl.BlockSpec(memory_space=pl.ANY)
    smem = pl.BlockSpec(memory_space=pltpu.SMEM)
    vmem = pl.BlockSpec(memory_space=pltpu.VMEM)
    audio = jax.ShapeDtypeStruct((heads, SLOTS, aud, HEAD_DIM), jnp.bfloat16)
    video = jax.ShapeDtypeStruct((heads, GROUP, vid, HEAD_DIM), jnp.bfloat16)
    return pl.pallas_call(
        lambda *refs: pair_kernel(nblocks, heads, *refs),
        in_specs=[smem, smem] + [anyspace] * 4,
        out_specs=[vmem] * 9,
        out_shape=[audio, audio, video, video]
        + result_shapes(vid, aud, heads)
        + [jax.ShapeDtypeStruct((8, HEAD_DIM), jnp.float32)],
        scratch_shapes=[
            pltpu.VMEM((SLOTS, aud, wide), jnp.bfloat16),
            pltpu.VMEM((GROUP, vid, wide), jnp.bfloat16),
            pltpu.VMEM((SLOTS, aud, wide), jnp.float32),
            pltpu.SemaphoreType.DMA((heads, 4, GROUP)),
            pltpu.SemaphoreType.DMA((heads, 4, GROUP)),
            pltpu.SemaphoreType.DMA((heads, 4)),
            pltpu.SemaphoreType.DMA((heads, 2, 2)),
            pltpu.SemaphoreType.DMA((heads, 2, 2)),
        ],
        compiler_params=pltpu.CompilerParams(
            collective_id=0, has_side_effects=True, vmem_limit_bytes=58 * 1024 * 1024
        ),
    )(bias, used, k, av, q, vv)


def safe_kernel(heads, bias, k, av, q, vv, o_ref, u_ref, halo_ref, log_ref, o_acc, u_acc, row_top, col_top):
    wide = o_acc.shape[-1]
    for t in range(heads):
        o_acc[...] = jnp.zeros_like(o_acc)
        u_acc[...] = jnp.zeros_like(u_acc)
        row_top[...] = jnp.full_like(row_top, NEG)
        col_top[...] = jnp.full_like(col_top, NEG)

        def update(acc, top, at, scores, values):
            old = top[at]
            new = jnp.maximum(old, jnp.max(scores, axis=1, keepdims=True))
            weights = jnp.exp(scores - new[:, :1]).astype(jnp.bfloat16)
            values = jnp.concatenate([values, jnp.ones_like(values)], axis=1)
            top[at] = new
            acc[at] = acc[at] * jnp.exp(old[:, :1] - new[:, :1]) + jnp.dot(
                weights, values, preferred_element_type=jnp.float32
            )

        def step(pair, carry):
            row = pair // SPAN
            col = row + pair % SPAN

            @pl.when(bias[pair] > -1.0)
            def _():
                query, keys = q[t, row], k[t, col]
                update(o_acc, row_top, row, dot_t(query, keys) * SCALE, av[t, col])
                update(u_acc, col_top, col, dot_t(keys, query) * SCALE, vv[t, row])

            return carry

        lax.fori_loop(0, GROUP * SPAN, step, 0)
        columns = slice(t * HEAD_DIM, (t + 1) * HEAD_DIM)
        for row in range(GROUP):
            o_ref[row, :, columns] = (o_acc[row, :, :HEAD_DIM] / o_acc[row, :, HEAD_DIM:]).astype(jnp.bfloat16)
        for slot in range(SLOTS):
            write_audio(
                t, slot, u_acc[slot, :, HEAD_DIM:], u_acc[slot, :, :HEAD_DIM], col_top[slot], u_ref, halo_ref, log_ref
            )


def safe_call(bias, k, av, q, vv):
    heads, _, vid, _ = q.shape
    aud = k.shape[2]
    wide = 2 * HEAD_DIM
    vmem = pl.BlockSpec(memory_space=pltpu.VMEM)
    return pl.pallas_call(
        lambda *refs: safe_kernel(heads, *refs),
        in_specs=[pl.BlockSpec(memory_space=pltpu.SMEM)] + [vmem] * 4,
        out_specs=[vmem] * 4,
        out_shape=result_shapes(vid, aud, heads),
        scratch_shapes=[
            pltpu.VMEM((GROUP, vid, wide), jnp.float32),
            pltpu.VMEM((SLOTS, aud, wide), jnp.float32),
            pltpu.VMEM((GROUP, vid, HEAD_DIM), jnp.float32),
            pltpu.VMEM((SLOTS, aud, HEAD_DIM), jnp.float32),
        ],
        compiler_params=pltpu.CompilerParams(vmem_limit_bytes=58 * 1024 * 1024),
    )(bias, k, av, q, vv)


def back_kernel(
    nblocks, width, o, u, halo, logs, video_proj, audio_proj, video_out, audio_out,
    o_out, u_out, wide_video, wide_audio, away_video, away_audio, there_video, there_audio,
    done, got, got_log, send, recv, local, zsend, zrecv, weight, csend, crecv,
):
    me, place, base, plane, planes = where_am_i(nblocks)
    core = lax.axis_index("head")
    heads = width // HEAD_DIM
    loads = [
        pltpu.make_async_copy(src, dst, weight.at[n])
        for n, (src, dst) in enumerate(((video_proj, wide_video), (audio_proj, wide_audio)))
    ]
    for load in loads:
        load.start()
    greet(place, base, plane, planes, 1 - core)
    up = [
        remote(halo.at[pl.ds(2, 2)], got.at[pl.ds(0, 2)], zsend.at[0, 0], zrecv.at[0, 0], me + GROUP),
        remote(logs.at[pl.ds(GROUP + 2, 2)], got_log.at[pl.ds(0, 2)], zsend.at[0, 1], zrecv.at[0, 1], me + GROUP),
    ]
    down = [
        remote(halo.at[pl.ds(0, 2)], got.at[pl.ds(2, 2)], zsend.at[1, 0], zrecv.at[1, 0], me - GROUP),
        remote(logs.at[pl.ds(GROUP, 2)], got_log.at[pl.ds(2, 2)], zsend.at[1, 1], zrecv.at[1, 1], me - GROUP),
    ]

    @pl.when(plane < planes - 1)
    def _():
        for copy in up:
            copy.start()

    @pl.when(plane > 0)
    def _():
        for copy in down:
            copy.start()

    columns = pl.ds(pl.multiple_of(place * width, width), width)
    copies = {}
    for d in (3, 1, 2):
        peer = place ^ d
        copies[0, d] = remote(o.at[peer], o_out.at[:, columns], send.at[0, d], recv.at[0, d], base + peer)
        copies[0, d].start()
    own = pltpu.make_async_copy(o.at[place], o_out.at[:, columns], local.at[0])
    own.start()

    @pl.when(plane > 0)
    def _():
        for copy in up:
            copy.wait_recv()

    @pl.when(plane == 0)
    def _():
        got[0:2] = jnp.zeros((2,) + got.shape[1:], jnp.bfloat16)
        got_log[0:2] = jnp.full((2,) + got_log.shape[1:], NEG, jnp.float32)

    @pl.when(plane < planes - 1)
    def _():
        for copy in down:
            copy.wait_recv()

    @pl.when(plane == planes - 1)
    def _():
        got[2:4] = jnp.zeros((2,) + got.shape[1:], jnp.bfloat16)
        got_log[2:4] = jnp.full((2,) + got_log.shape[1:], NEG, jnp.float32)

    for slot in range(GROUP):
        for h in range(heads):
            cols = slice(h * HEAD_DIM, (h + 1) * HEAD_DIM)
            first, second = logs[slot, h], got_log[slot, h]
            top = jnp.maximum(first, second)
            a, b = jnp.exp(first - top), jnp.exp(second - top)
            share = a / (a + b)
            share = jnp.transpose(jnp.concatenate([share] * (HEAD_DIM // 8), axis=0))
            there = got[slot, :, cols].astype(jnp.float32)
            done[slot, :, cols] = (there + share * (u[slot, :, cols] - there)).astype(jnp.bfloat16)
    for d in (3, 1, 2):
        peer = place ^ d
        copies[1, d] = remote(done.at[peer], u_out.at[:, columns], send.at[1, d], recv.at[1, d], base + peer)
        copies[1, d].start()
    own_u = pltpu.make_async_copy(done.at[place], u_out.at[:, columns], local.at[1])
    own_u.start()
    half = video_out.shape[1]
    tiles = half // TILE

    def columns_of(who, tile):
        return pl.ds(pl.multiple_of(who * half + tile * TILE, TILE), TILE)

    def project(n, attn, weights, away, there, out):
        def passing(tile):
            columns = pl.ds(pl.multiple_of(tile * TILE, TILE), TILE)
            return pltpu.make_async_remote_copy(
                src_ref=away.at[:, columns],
                dst_ref=there.at[:, columns],
                send_sem=csend.at[n, tile],
                recv_sem=crecv.at[n, tile],
                device_id={"head": 1 - core},
                device_id_type=LOGICAL,
            )

        def theirs(tile, carry):
            away[:, pl.ds(pl.multiple_of(tile * TILE, TILE), TILE)] = jnp.dot(
                attn[...], weights[:, columns_of(1 - core, tile)], preferred_element_type=jnp.float32
            )
            passing(tile).start()
            return carry

        def mine(tile, carry):
            columns = pl.ds(pl.multiple_of(tile * TILE, TILE), TILE)
            part = jnp.dot(attn[...], weights[:, columns_of(core, tile)], preferred_element_type=jnp.float32)
            passing(tile).wait_recv()
            out[:, columns] = (part + there[:, columns]).astype(jnp.bfloat16)
            passing(tile).wait_send()
            return carry

        lax.fori_loop(0, tiles, theirs, 0)
        lax.fori_loop(0, tiles, mine, 0)

    own.wait()
    loads[0].wait()
    for d in range(1, GROUP):
        copies[0, d].wait_recv()
    project(0, o_out, wide_video, away_video, there_video, video_out)
    own_u.wait()
    loads[1].wait()
    for d in range(1, GROUP):
        copies[1, d].wait_recv()
    project(1, u_out, wide_audio, away_audio, there_audio, audio_out)
    for copy in copies.values():
        copy.wait_send()

    @pl.when(plane < planes - 1)
    def _():
        for copy in up:
            copy.wait_send()

    @pl.when(plane > 0)
    def _():
        for copy in down:
            copy.wait_send()


def give_back(o, u, halo, logs, video_proj, audio_proj, nblocks):
    vid, aud, width = o.shape[1], u.shape[1], o.shape[2]
    half = video_proj.shape[1] // 2
    anyspace = pl.BlockSpec(memory_space=pl.ANY)
    vmem = pl.BlockSpec(memory_space=pltpu.VMEM)
    return pl.pallas_call(
        lambda *refs: back_kernel(nblocks, width, *refs),
        in_specs=[anyspace, vmem, vmem, vmem, anyspace, anyspace],
        out_specs=[vmem] * 2,
        out_shape=[
            jax.ShapeDtypeStruct((vid, half), jnp.bfloat16),
            jax.ShapeDtypeStruct((aud, half), jnp.bfloat16),
        ],
        scratch_shapes=[
            pltpu.VMEM((vid, GROUP * width), jnp.bfloat16),
            pltpu.VMEM((aud, GROUP * width), jnp.bfloat16),
            pltpu.VMEM(video_proj.shape, jnp.bfloat16),
            pltpu.VMEM(audio_proj.shape, jnp.bfloat16),
            pltpu.VMEM((vid, half), jnp.float32),
            pltpu.VMEM((aud, half), jnp.float32),
            pltpu.VMEM((vid, half), jnp.float32),
            pltpu.VMEM((aud, half), jnp.float32),
            pltpu.VMEM((GROUP, aud, width), jnp.bfloat16),
            pltpu.VMEM((GROUP, aud, width), jnp.bfloat16),
            pltpu.VMEM((GROUP,) + logs.shape[1:], jnp.float32),
            pltpu.SemaphoreType.DMA((2, GROUP)),
            pltpu.SemaphoreType.DMA((2, GROUP)),
            pltpu.SemaphoreType.DMA((2,)),
            pltpu.SemaphoreType.DMA((2, 2)),
            pltpu.SemaphoreType.DMA((2, 2)),
            pltpu.SemaphoreType.DMA((2,)),
            pltpu.SemaphoreType.DMA((2, half // TILE)),
            pltpu.SemaphoreType.DMA((2, half // TILE)),
        ],
        compiler_params=pltpu.CompilerParams(
            collective_id=1, has_side_effects=True, vmem_limit_bytes=58 * 1024 * 1024
        ),
    )(o, u, halo, logs, video_proj, audio_proj)


def shards(
    video_query, video_value, audio_key, audio_value, video_proj, audio_proj, pair_first, pair_count
):
    nblocks = lax.axis_size("seq")
    me = lax.axis_index("seq")
    base = me - me % GROUP
    offsets = jnp.arange(SPAN)[None, :] - HALF + base + jnp.arange(GROUP)[:, None]
    first = lax.dynamic_slice_in_dim(pair_first, base, GROUP)[:, None]
    count = lax.dynamic_slice_in_dim(pair_count, base, GROUP)[:, None]
    valid = (offsets >= first) & (offsets < first + count)
    bias = jnp.where(valid, 0.0, NEG).astype(jnp.float32).reshape(-1)
    audio_blocks = base - HALF + jnp.arange(SLOTS)[None, :]
    used = jnp.any((audio_blocks >= first) & (audio_blocks < first + count), axis=0).astype(jnp.float32)
    *held, o, u, halo, logs, bad = pair_call(
        bias, used, audio_key, audio_value, video_query, video_value, nblocks
    )
    o, u, halo, logs = lax.cond(
        jnp.max(bad) > 0, lambda: tuple(safe_call(bias, *held)), lambda: (o, u, halo, logs)
    )
    return tuple(give_back(o, u, halo, logs, video_proj, audio_proj, nblocks))


def solution(mesh):
    in_specs = (
        P("seq", "head"),
        P("seq", "head"),
        P("seq", "head"),
        P("seq", "head"),
        P("head", None),
        P("head", None),
        P(),
        P(),
    )
    out_specs = (P("seq", "head"), P("seq", "head"))
    return jax.shard_map(shards, mesh=mesh, in_specs=in_specs, out_specs=out_specs, check_vma=False)
```

```python
import math

import jax
import jax.numpy as jnp
from jax import lax
from jax.experimental import pallas as pl
from jax.experimental.pallas import tpu as pltpu
from jax.sharding import PartitionSpec as P

HEAD_DIM = 128
GROUP = 4
HALF = 2
NEG = -1e30
SCALE = 1.0 / math.sqrt(HEAD_DIM)
LOG2E = 1.4426950408889634
LOW, HIGH = 1e-25, 1e25
LOGICAL = pl.DeviceIdType.MESH


def shifted(x, axis, by):
    size = lax.axis_size(axis)
    pairs = [(i, i + by) for i in range(size) if 0 <= i + by < size]
    return lax.ppermute(x, axis, pairs)


def tile_scores(query, keys):
    return jnp.einsum("vhe,ahe->hva", query, keys, preferred_element_type=jnp.float32) / math.sqrt(
        HEAD_DIM
    )


def row_piece(scores, values):
    top = jnp.max(scores, axis=2)
    expo = jnp.exp(scores - top[:, :, None])
    total = jnp.sum(expo, axis=2)
    out = jnp.einsum(
        "hva,ahe->vhe", expo.astype(jnp.bfloat16), values, preferred_element_type=jnp.float32
    )
    return (top, total, out)


def col_piece(scores, values):
    top = jnp.max(scores, axis=1)
    expo = jnp.exp(scores - top[:, None, :])
    total = jnp.sum(expo, axis=1)
    out = jnp.einsum(
        "hva,vhe->ahe", expo.astype(jnp.bfloat16), values, preferred_element_type=jnp.float32
    )
    return (top, total, out)


def combine(acc, part):
    top_a, total_a, out_a = acc
    top_b, total_b, out_b = part
    top = jnp.maximum(top_a, top_b)
    old = jnp.exp(top_a - top)
    new = jnp.exp(top_b - top)
    return (
        top,
        total_a * old + total_b * new,
        out_a * old.T[:, :, None] + out_b * new.T[:, :, None],
    )


def empty_acc(heads, rows):
    return (
        jnp.full((heads, rows), NEG, jnp.float32),
        jnp.zeros((heads, rows), jnp.float32),
        jnp.zeros((rows, heads, HEAD_DIM), jnp.float32),
    )


def finish(acc):
    top, total, out = acc
    result = (out / total.T[:, :, None]).astype(jnp.bfloat16)
    return result.reshape(result.shape[0], result.shape[1] * result.shape[2])


def safe_shards(
    video_query, video_value, audio_key, audio_value, video_proj, audio_proj, pair_first, pair_count
):
    heads = video_query.shape[1] // HEAD_DIM
    vid = video_query.shape[0]
    aud = audio_key.shape[0]
    nblocks = lax.axis_size("seq")
    me = lax.axis_index("seq")
    first = pair_first[me]
    count = pair_count[me]
    query = video_query.reshape(vid, heads, HEAD_DIM)
    own_keys = audio_key.reshape(aud, heads, HEAD_DIM)
    audio_pair = jnp.stack([audio_key, audio_value])
    video_pair = jnp.stack([video_query, video_value])
    video_acc = empty_acc(heads, vid)
    audio_acc = empty_acc(heads, aud)
    for offset in range(-HALF, HALF + 1):
        if offset == 0:
            arrived = audio_pair
        else:
            arrived = shifted(audio_pair, "seq", -offset)
        keys = arrived[0].reshape(aud, heads, HEAD_DIM)
        aud_vals = arrived[1].reshape(aud, heads, HEAD_DIM)
        target = me + offset
        valid = (target >= first) & (target < first + count)
        source = me - offset
        clipped = jnp.clip(source, 0, nblocks - 1)
        from_source = (
            (source >= 0)
            & (source < nblocks)
            & (pair_first[clipped] <= me)
            & (me < pair_first[clipped] + pair_count[clipped])
        )

        def video_side(unused):
            return row_piece(tile_scores(query, keys), aud_vals)

        def no_video(unused):
            return empty_acc(heads, vid)

        video_acc = combine(video_acc, lax.cond(valid, video_side, no_video, 0))
        if offset == 0:
            visiting = video_pair
        else:
            visiting = shifted(video_pair, "seq", offset)

        def audio_side(unused):
            visit_query = visiting[0].reshape(vid, heads, HEAD_DIM)
            visit_vals = visiting[1].reshape(vid, heads, HEAD_DIM)
            return col_piece(tile_scores(visit_query, own_keys), visit_vals)

        def no_audio(unused):
            return empty_acc(heads, aud)

        audio_acc = combine(audio_acc, lax.cond(from_source, audio_side, no_audio, 0))
    video_attn = finish(video_acc)
    audio_attn = finish(audio_acc)
    video_term = jnp.dot(video_attn, video_proj, preferred_element_type=jnp.float32)
    audio_term = jnp.dot(audio_attn, audio_proj, preferred_element_type=jnp.float32)
    video_sum, audio_sum = (
        lax.psum_scatter(video_term, "head", scatter_dimension=1, tiled=True),
        lax.psum_scatter(audio_term, "head", scatter_dimension=1, tiled=True),
    )
    return (video_sum.astype(jnp.bfloat16), audio_sum.astype(jnp.bfloat16))


def greet(place, base, plane, planes, core):
    barrier = pltpu.get_barrier_semaphore()
    for d in range(1, GROUP):
        pl.semaphore_signal(barrier, inc=1, device_id={"seq": base + (place ^ d)}, device_id_type=LOGICAL)
    for e in range(1, planes):
        target = lax.rem(plane + e, planes) * GROUP + place
        pl.semaphore_signal(barrier, inc=1, device_id={"seq": target}, device_id_type=LOGICAL)
    pl.semaphore_signal(barrier, inc=1, device_id={"head": 1 - core}, device_id_type=LOGICAL)
    pl.semaphore_wait(barrier, GROUP + planes - 1)


def where_am_i(nblocks):
    me = lax.axis_index("seq")
    place = lax.rem(me, GROUP)
    return me, place, me - place, me // GROUP, nblocks // GROUP


def remote(src, dst, send, recv, target):
    return pltpu.make_async_remote_copy(
        src_ref=src, dst_ref=dst, send_sem=send, recv_sem=recv, device_id={"seq": target}, device_id_type=LOGICAL
    )


TILE = 512
SPAN = 2 * HALF + 1
SLOTS = GROUP + 2 * HALF
OWN = (4, 5, 0, 1, 2, 3, 6, 7)


def dot_t(a, b):
    return lax.dot_general(a, b, (((1,), (1,)), ((), ())), preferred_element_type=jnp.float32)


def write_audio(t, slot, total, summed, top, u_ref, halo_ref, log_ref):
    some = total > 0
    mean = jnp.where(some, summed / jnp.where(some, total, 1.0), 0.0)
    logs = jnp.where(some, top + jnp.log(jnp.where(some, total, 1.0)), NEG)
    place = OWN[slot]
    columns = slice(t * HEAD_DIM, (t + 1) * HEAD_DIM)
    if place < GROUP:
        u_ref[place, :, columns] = mean
    else:
        halo_ref[place - GROUP, :, columns] = mean.astype(jnp.bfloat16)
    log_ref[place, t] = jnp.transpose(logs)[:8]


def whole_kernel(
    nblocks, heads, bias, used, k, av, q, vv, video_proj, audio_proj,
    video_out, audio_out, bad_out,
    k_buf, av_buf, q_buf, vv_buf, o_ref, u_ref, halo_ref, log_ref, bad_ref,
    avx, vvx, u_acc, video_attn, audio_attn, wide_video, wide_audio,
    away_video, away_audio, there_video, there_audio, done, got, got_log, flag_out, flag_in,
    send, recv, local, zsend, zrecv, bsend, brecv, blocal, rsend, rrecv,
    weight, csend, crecv, fsend, frecv,
):
    me, place, base, plane, planes = where_am_i(nblocks)
    core = lax.axis_index("head")
    vid, aud = q.shape[0], k.shape[0]
    greet(place, base, plane, planes, core)
    arrays = ((k, k_buf, HALF), (av, av_buf, HALF), (q, q_buf, 0), (vv, vv_buf, 0))

    def column(member, t):
        return pl.ds(pl.multiple_of((member * heads + t) * HEAD_DIM, HEAD_DIM), HEAD_DIM)

    copies, own = {}, {}
    for t in range(heads):
        for n, (src, dst, at) in enumerate(arrays):
            for d in (3, 1, 2):
                peer = place ^ d
                copies[t, n, d] = remote(
                    src.at[:, column(peer, t)], dst.at[t, place + at], send.at[t, n, d], recv.at[t, n, d], base + peer
                )
                copies[t, n, d].start()
    for t in range(heads):
        for n, (src, dst, at) in enumerate(arrays):
            own[t, n] = pltpu.make_async_copy(src.at[:, column(place, t)], dst.at[t, place + at], local.at[t, n])
            own[t, n].start()

    loads = [
        pltpu.make_async_copy(src, dst, weight.at[n])
        for n, (src, dst) in enumerate(((video_proj, wide_video), (audio_proj, wide_audio)))
    ]
    for load in loads:
        load.start()

    def returns(t, up):
        source, target = (HALF, 0) if up else (0, HALF)
        side = 0 if up else 1
        columns = slice(t * HEAD_DIM, (t + 1) * HEAD_DIM)
        pairs = (
            (halo_ref.at[pl.ds(source, HALF), :, columns], got.at[pl.ds(target, HALF), :, columns]),
            (log_ref.at[pl.ds(GROUP + source, HALF), t], got_log.at[pl.ds(target, HALF), t]),
        )
        return [
            remote(src, dst, rsend.at[t, side, n], rrecv.at[t, side, n], me + GROUP if up else me - GROUP)
            for n, (src, dst) in enumerate(pairs)
        ]

    def backs(n, t):
        src, dst = ((o_ref, video_attn), (done, audio_attn))[n]
        columns = slice(t * HEAD_DIM, (t + 1) * HEAD_DIM)
        return [
            remote(
                src.at[place ^ d, :, columns],
                dst.at[:, column(place, t)],
                bsend.at[n, t, d],
                brecv.at[n, t, d],
                base + (place ^ d),
            )
            for d in (3, 1, 2)
        ], pltpu.make_async_copy(src.at[place, :, columns], dst.at[:, column(place, t)], blocal.at[n, t])

    def start_back(n, t):
        away, stay = backs(n, t)
        for copy in away:
            copy.start()
        stay.start()

    def wait_back(n):
        for t in range(heads):
            away, stay = backs(n, t)
            for copy in away:
                copy.wait_recv()
            stay.wait()

    def finish_audio(t):
        @pl.when(plane > 0)
        def _():
            for copy in returns(t, True):
                copy.wait_recv()

        @pl.when(plane < planes - 1)
        def _():
            for copy in returns(t, False):
                copy.wait_recv()

        columns = slice(t * HEAD_DIM, (t + 1) * HEAD_DIM)
        for slot in range(GROUP):
            first, second = log_ref[slot, t], got_log[slot, t]
            top = jnp.maximum(first, second)
            a, b = jnp.exp(first - top), jnp.exp(second - top)
            share = a / (a + b)
            share = jnp.transpose(jnp.concatenate([share] * (HEAD_DIM // 8), axis=0))
            there = got[slot, :, columns].astype(jnp.float32)
            done[slot, :, columns] = (there + share * (u_ref[slot, :, columns] - there)).astype(jnp.bfloat16)
        start_back(1, t)

    def relays(t, up):
        source, target = (GROUP, 0) if up else (HALF, GROUP + HALF)
        side = 0 if up else 1
        return [
            remote(
                x.at[t, pl.ds(source, HALF)],
                x.at[t, pl.ds(target, HALF)],
                zsend.at[t, side, n],
                zrecv.at[t, side, n],
                me + GROUP if up else me - GROUP,
            )
            for n, x in enumerate((k_buf, av_buf))
        ]

    avx[:, :, HEAD_DIM:] = jnp.ones((SLOTS, aud, HEAD_DIM), jnp.bfloat16)
    vvx[:, :, HEAD_DIM:] = jnp.ones((GROUP, vid, HEAD_DIM), jnp.bfloat16)

    @pl.when(plane == 0)
    def _():
        for x in (k_buf, av_buf):
            x[:, :HALF] = jnp.zeros((heads, HALF, aud, HEAD_DIM), jnp.bfloat16)

    @pl.when(plane == planes - 1)
    def _():
        for x in (k_buf, av_buf):
            x[:, GROUP + HALF :] = jnp.zeros((heads, HALF, aud, HEAD_DIM), jnp.bfloat16)

    def outside(total):
        wrong = jnp.where((total >= LOW) & (total <= HIGH), 0.0, 1.0)
        return jnp.max(wrong.reshape(-1, 8, HEAD_DIM), axis=0)

    @pl.when(plane == 0)
    def _():
        got[:HALF] = jnp.zeros((HALF,) + got.shape[1:], jnp.bfloat16)
        got_log[:HALF] = jnp.full((HALF,) + got_log.shape[1:], NEG, jnp.float32)

    @pl.when(plane == planes - 1)
    def _():
        got[HALF:] = jnp.zeros((HALF,) + got.shape[1:], jnp.bfloat16)
        got_log[HALF:] = jnp.full((HALF,) + got_log.shape[1:], NEG, jnp.float32)

    bad_ref[...] = jnp.zeros_like(bad_ref)
    for t in range(heads):
        for n in range(4):
            own[t, n].wait()
            for d in range(1, GROUP):
                copies[t, n, d].wait_recv()
            if n == 1:

                @pl.when(plane < planes - 1)
                def _():
                    for copy in relays(t, True):
                        copy.start()

                @pl.when(plane > 0)
                def _():
                    for copy in relays(t, False):
                        copy.start()

        @pl.when(plane < planes - 1)
        def _():
            for copy in relays(t, False):
                copy.wait_recv()

        @pl.when(plane > 0)
        def _():
            for copy in relays(t, True):
                copy.wait_recv()

        avx[:, :, :HEAD_DIM] = av_buf[t]
        vvx[:, :, :HEAD_DIM] = vv_buf[t]
        u_acc[...] = jnp.zeros_like(u_acc)
        columns = slice(t * HEAD_DIM, (t + 1) * HEAD_DIM)

        def step(row, carry):
            query = q_buf[t, row]
            weights = jnp.concatenate(
                [
                    jnp.exp2(
                        dot_t(query, k_buf[t, row + c]) * (SCALE * LOG2E) + bias[row * SPAN + c]
                    ).astype(jnp.bfloat16)
                    for c in range(SPAN)
                ],
                axis=1,
            )
            values = avx[pl.ds(row, SPAN)].reshape(SPAN * aud, 2 * HEAD_DIM)
            out = jnp.dot(weights, values, preferred_element_type=jnp.float32)
            total = out[:, HEAD_DIM:]
            o_ref[row, :, columns] = (out[:, :HEAD_DIM] / total).astype(jnp.bfloat16)
            bad_ref[...] = jnp.maximum(bad_ref[...], outside(total))
            back = lax.dot_general(
                weights, vvx[row], (((0,), (0,)), ((), ())), preferred_element_type=jnp.float32
            )
            u_acc[pl.ds(row, SPAN)] += back.reshape(SPAN, aud, 2 * HEAD_DIM)
            return carry

        lax.fori_loop(0, GROUP, step, 0)
        for slot in range(SLOTS):
            total = u_acc[slot, :, HEAD_DIM:]
            bad_ref[...] = jnp.maximum(bad_ref[...], outside(total) * used[slot])
            write_audio(t, slot, total, u_acc[slot, :, :HEAD_DIM], 0.0, u_ref, halo_ref, log_ref)
        start_back(0, t)

        @pl.when(plane < planes - 1)
        def _():
            for copy in returns(t, True):
                copy.start()

        @pl.when(plane > 0)
        def _():
            for copy in returns(t, False):
                copy.start()

        if t > 0:
            finish_audio(t - 1)

    def flags(stage):
        lines = [{"seq": lax.rem(plane + e, planes) * GROUP + place} for e in range(1, planes)]
        peers = [{"seq": base + (place ^ d)} for d in range(1, GROUP)]
        at, targets = ((0, lines), (planes - 1, peers), (planes + GROUP - 2, [{"head": 1 - core}]))[stage]
        return at, [
            pltpu.make_async_remote_copy(
                src_ref=flag_out.at[stage],
                dst_ref=flag_in.at[at + n],
                send_sem=fsend.at[at + n],
                recv_sem=frecv.at[at + n],
                device_id=target,
                device_id_type=LOGICAL,
            )
            for n, target in enumerate(targets)
        ]

    def start_flags(stage):
        flag_out[stage] = bad_ref[...]
        for copy in flags(stage)[1]:
            copy.start()

    def end_flags(stage):
        at, sent = flags(stage)
        for n, copy in enumerate(sent):
            copy.wait()
            bad_ref[...] = jnp.maximum(bad_ref[...], flag_in[at + n])

    start_flags(0)
    finish_audio(heads - 1)
    half = video_out.shape[1]
    tiles = half // TILE

    def columns_of(who, tile):
        return pl.ds(pl.multiple_of(who * half + tile * TILE, TILE), TILE)

    def project(n, attn, weights, away, there, out):
        def passing(tile):
            columns = pl.ds(pl.multiple_of(tile * TILE, TILE), TILE)
            return pltpu.make_async_remote_copy(
                src_ref=away.at[:, columns],
                dst_ref=there.at[:, columns],
                send_sem=csend.at[n, tile],
                recv_sem=crecv.at[n, tile],
                device_id={"head": 1 - core},
                device_id_type=LOGICAL,
            )

        def theirs(tile, carry):
            away[:, pl.ds(pl.multiple_of(tile * TILE, TILE), TILE)] = jnp.dot(
                attn[...], weights[:, columns_of(1 - core, tile)], preferred_element_type=jnp.float32
            )
            passing(tile).start()
            return carry

        def mine(tile, carry):
            columns = pl.ds(pl.multiple_of(tile * TILE, TILE), TILE)
            part = jnp.dot(attn[...], weights[:, columns_of(core, tile)], preferred_element_type=jnp.float32)
            passing(tile).wait_recv()
            out[:, columns] = (part + there[:, columns]).astype(jnp.bfloat16)
            passing(tile).wait_send()
            return carry

        lax.fori_loop(0, tiles, theirs, 0)
        lax.fori_loop(0, tiles, mine, 0)

    end_flags(0)
    start_flags(1)
    loads[0].wait()
    wait_back(0)
    project(0, video_attn, wide_video, away_video, there_video, video_out)
    end_flags(1)
    start_flags(2)
    loads[1].wait()
    wait_back(1)
    project(1, audio_attn, wide_audio, away_audio, there_audio, audio_out)
    end_flags(2)
    bad_out[...] = bad_ref[...]
    for copy in copies.values():
        copy.wait_send()
    for n in range(2):
        for t in range(heads):
            for copy in backs(n, t)[0]:
                copy.wait_send()

    @pl.when(plane < planes - 1)
    def _():
        for t in range(heads):
            for copy in relays(t, True) + returns(t, True):
                copy.wait_send()

    @pl.when(plane > 0)
    def _():
        for t in range(heads):
            for copy in relays(t, False) + returns(t, False):
                copy.wait_send()


def whole_call(bias, used, k, av, q, vv, video_proj, audio_proj, nblocks):
    vid, aud = q.shape[0], k.shape[0]
    heads = q.shape[1] // HEAD_DIM // GROUP
    width = heads * HEAD_DIM
    wide = 2 * HEAD_DIM
    half = video_proj.shape[1] // 2
    planes = nblocks // GROUP
    messages = planes - 1 + GROUP
    anyspace = pl.BlockSpec(memory_space=pl.ANY)
    smem = pl.BlockSpec(memory_space=pltpu.SMEM)
    vmem = pl.BlockSpec(memory_space=pltpu.VMEM)
    bf16, f32, dma = jnp.bfloat16, jnp.float32, pltpu.SemaphoreType.DMA
    return pl.pallas_call(
        lambda *refs: whole_kernel(nblocks, heads, *refs),
        in_specs=[smem, smem] + [anyspace] * 6,
        out_specs=[vmem] * 3,
        out_shape=[
            jax.ShapeDtypeStruct((vid, half), bf16),
            jax.ShapeDtypeStruct((aud, half), bf16),
            jax.ShapeDtypeStruct((8, HEAD_DIM), f32),
        ],
        scratch_shapes=[
            pltpu.VMEM((heads, SLOTS, aud, HEAD_DIM), bf16),
            pltpu.VMEM((heads, SLOTS, aud, HEAD_DIM), bf16),
            pltpu.VMEM((heads, GROUP, vid, HEAD_DIM), bf16),
            pltpu.VMEM((heads, GROUP, vid, HEAD_DIM), bf16),
            pltpu.VMEM((GROUP, vid, width), bf16),
            pltpu.VMEM((GROUP, aud, width), f32),
            pltpu.VMEM((GROUP, aud, width), bf16),
            pltpu.VMEM((SLOTS, heads, 8, aud), f32),
            pltpu.VMEM((8, HEAD_DIM), f32),
            pltpu.VMEM((SLOTS, aud, wide), bf16),
            pltpu.VMEM((GROUP, vid, wide), bf16),
            pltpu.VMEM((SLOTS, aud, wide), f32),
            pltpu.VMEM((vid, GROUP * width), bf16),
            pltpu.VMEM((aud, GROUP * width), bf16),
            pltpu.VMEM(video_proj.shape, bf16),
            pltpu.VMEM(audio_proj.shape, bf16),
            pltpu.VMEM((vid, half), f32),
            pltpu.VMEM((aud, half), f32),
            pltpu.VMEM((vid, half), f32),
            pltpu.VMEM((aud, half), f32),
            pltpu.VMEM((GROUP, aud, width), bf16),
            pltpu.VMEM((GROUP, aud, width), bf16),
            pltpu.VMEM((GROUP, heads, 8, aud), f32),
            pltpu.VMEM((3, 8, HEAD_DIM), f32),
            pltpu.VMEM((messages, 8, HEAD_DIM), f32),
            dma((heads, 4, GROUP)),
            dma((heads, 4, GROUP)),
            dma((heads, 4)),
            dma((heads, 2, 2)),
            dma((heads, 2, 2)),
            dma((2, heads, GROUP)),
            dma((2, heads, GROUP)),
            dma((2, heads)),
            dma((heads, 2, 2)),
            dma((heads, 2, 2)),
            dma((2,)),
            dma((2, half // TILE)),
            dma((2, half // TILE)),
            dma((messages,)),
            dma((messages,)),
        ],
        compiler_params=pltpu.CompilerParams(
            collective_id=0, has_side_effects=True, vmem_limit_bytes=60 * 1024 * 1024
        ),
    )(bias, used, k, av, q, vv, video_proj, audio_proj)


def shards(
    video_query, video_value, audio_key, audio_value, video_proj, audio_proj, pair_first, pair_count
):
    nblocks = lax.axis_size("seq")
    me = lax.axis_index("seq")
    base = me - me % GROUP
    offsets = jnp.arange(SPAN)[None, :] - HALF + base + jnp.arange(GROUP)[:, None]
    first = lax.dynamic_slice_in_dim(pair_first, base, GROUP)[:, None]
    count = lax.dynamic_slice_in_dim(pair_count, base, GROUP)[:, None]
    valid = (offsets >= first) & (offsets < first + count)
    bias = jnp.where(valid, 0.0, NEG).astype(jnp.float32).reshape(-1)
    audio_blocks = base - HALF + jnp.arange(SLOTS)[None, :]
    used = jnp.any((audio_blocks >= first) & (audio_blocks < first + count), axis=0).astype(jnp.float32)
    video_out, audio_out, bad = whole_call(
        bias, used, audio_key, audio_value, video_query, video_value, video_proj, audio_proj, nblocks
    )
    arguments = (
        video_query, video_value, audio_key, audio_value, video_proj, audio_proj, pair_first, pair_count
    )
    return lax.cond(
        jnp.max(bad) > 0, lambda: safe_shards(*arguments), lambda: (video_out, audio_out)
    )


def solution(mesh):
    in_specs = (
        P("seq", "head"),
        P("seq", "head"),
        P("seq", "head"),
        P("seq", "head"),
        P("head", None),
        P("head", None),
        P(),
        P(),
    )
    out_specs = (P("seq", "head"), P("seq", "head"))
    return jax.shard_map(shards, mesh=mesh, in_specs=in_specs, out_specs=out_specs, check_vma=False)
```

```python
import math

import jax
import jax.numpy as jnp
from jax import lax
from jax.experimental import pallas as pl
from jax.experimental.pallas import tpu as pltpu
from jax.sharding import PartitionSpec as P

HEAD_DIM = 128
GROUP = 4
HALF = 2
NEG = -1e30
SCALE = 1.0 / math.sqrt(HEAD_DIM)
LOG2E = 1.4426950408889634
LOW, HIGH = 1e-25, 1e25
LOGICAL = pl.DeviceIdType.MESH


def shifted(x, axis, by):
    size = lax.axis_size(axis)
    pairs = [(i, i + by) for i in range(size) if 0 <= i + by < size]
    return lax.ppermute(x, axis, pairs)


def tile_scores(query, keys):
    return jnp.einsum("vhe,ahe->hva", query, keys, preferred_element_type=jnp.float32) / math.sqrt(
        HEAD_DIM
    )


def row_piece(scores, values):
    top = jnp.max(scores, axis=2)
    expo = jnp.exp(scores - top[:, :, None])
    total = jnp.sum(expo, axis=2)
    out = jnp.einsum(
        "hva,ahe->vhe", expo.astype(jnp.bfloat16), values, preferred_element_type=jnp.float32
    )
    return (top, total, out)


def col_piece(scores, values):
    top = jnp.max(scores, axis=1)
    expo = jnp.exp(scores - top[:, None, :])
    total = jnp.sum(expo, axis=1)
    out = jnp.einsum(
        "hva,vhe->ahe", expo.astype(jnp.bfloat16), values, preferred_element_type=jnp.float32
    )
    return (top, total, out)


def combine(acc, part):
    top_a, total_a, out_a = acc
    top_b, total_b, out_b = part
    top = jnp.maximum(top_a, top_b)
    old = jnp.exp(top_a - top)
    new = jnp.exp(top_b - top)
    return (
        top,
        total_a * old + total_b * new,
        out_a * old.T[:, :, None] + out_b * new.T[:, :, None],
    )


def empty_acc(heads, rows):
    return (
        jnp.full((heads, rows), NEG, jnp.float32),
        jnp.zeros((heads, rows), jnp.float32),
        jnp.zeros((rows, heads, HEAD_DIM), jnp.float32),
    )


def finish(acc):
    top, total, out = acc
    result = (out / total.T[:, :, None]).astype(jnp.bfloat16)
    return result.reshape(result.shape[0], result.shape[1] * result.shape[2])


def safe_shards(
    video_query, video_value, audio_key, audio_value, video_proj, audio_proj, pair_first, pair_count
):
    heads = video_query.shape[1] // HEAD_DIM
    vid = video_query.shape[0]
    aud = audio_key.shape[0]
    nblocks = lax.axis_size("seq")
    me = lax.axis_index("seq")
    first = pair_first[me]
    count = pair_count[me]
    query = video_query.reshape(vid, heads, HEAD_DIM)
    own_keys = audio_key.reshape(aud, heads, HEAD_DIM)
    audio_pair = jnp.stack([audio_key, audio_value])
    video_pair = jnp.stack([video_query, video_value])
    video_acc = empty_acc(heads, vid)
    audio_acc = empty_acc(heads, aud)
    for offset in range(-HALF, HALF + 1):
        if offset == 0:
            arrived = audio_pair
        else:
            arrived = shifted(audio_pair, "seq", -offset)
        keys = arrived[0].reshape(aud, heads, HEAD_DIM)
        aud_vals = arrived[1].reshape(aud, heads, HEAD_DIM)
        target = me + offset
        valid = (target >= first) & (target < first + count)
        source = me - offset
        clipped = jnp.clip(source, 0, nblocks - 1)
        from_source = (
            (source >= 0)
            & (source < nblocks)
            & (pair_first[clipped] <= me)
            & (me < pair_first[clipped] + pair_count[clipped])
        )

        def video_side(unused):
            return row_piece(tile_scores(query, keys), aud_vals)

        def no_video(unused):
            return empty_acc(heads, vid)

        video_acc = combine(video_acc, lax.cond(valid, video_side, no_video, 0))
        if offset == 0:
            visiting = video_pair
        else:
            visiting = shifted(video_pair, "seq", offset)

        def audio_side(unused):
            visit_query = visiting[0].reshape(vid, heads, HEAD_DIM)
            visit_vals = visiting[1].reshape(vid, heads, HEAD_DIM)
            return col_piece(tile_scores(visit_query, own_keys), visit_vals)

        def no_audio(unused):
            return empty_acc(heads, aud)

        audio_acc = combine(audio_acc, lax.cond(from_source, audio_side, no_audio, 0))
    video_attn = finish(video_acc)
    audio_attn = finish(audio_acc)
    video_term = jnp.dot(video_attn, video_proj, preferred_element_type=jnp.float32)
    audio_term = jnp.dot(audio_attn, audio_proj, preferred_element_type=jnp.float32)
    half = video_proj.shape[1] // 2
    core = lax.axis_index("head")

    def total(term):
        away = lax.dynamic_slice_in_dim(term, (1 - core) * half, half, 1)
        mine = lax.dynamic_slice_in_dim(term, core * half, half, 1)
        return (mine + lax.ppermute(away, "head", [(0, 1), (1, 0)])).astype(jnp.bfloat16)

    return (total(video_term), total(audio_term))


def greet(place, base, plane, planes, core):
    barrier = pltpu.get_barrier_semaphore()
    for d in range(1, GROUP):
        pl.semaphore_signal(barrier, inc=1, device_id={"seq": base + (place ^ d)}, device_id_type=LOGICAL)
    for e in range(1, planes):
        target = lax.rem(plane + e, planes) * GROUP + place
        pl.semaphore_signal(barrier, inc=1, device_id={"seq": target}, device_id_type=LOGICAL)
    pl.semaphore_signal(barrier, inc=1, device_id={"head": 1 - core}, device_id_type=LOGICAL)
    pl.semaphore_wait(barrier, GROUP + planes - 1)


def where_am_i(nblocks):
    me = lax.axis_index("seq")
    place = lax.rem(me, GROUP)
    return me, place, me - place, me // GROUP, nblocks // GROUP


def remote(src, dst, send, recv, target):
    return pltpu.make_async_remote_copy(
        src_ref=src, dst_ref=dst, send_sem=send, recv_sem=recv, device_id={"seq": target}, device_id_type=LOGICAL
    )


TILE = 512
SPAN = 2 * HALF + 1
SLOTS = GROUP + 2 * HALF
OWN = (4, 5, 0, 1, 2, 3, 6, 7)


def dot_t(a, b):
    return lax.dot_general(a, b, (((1,), (1,)), ((), ())), preferred_element_type=jnp.float32)


def write_audio(t, slot, total, summed, top, u_ref, halo_ref, log_ref):
    some = total > 0
    mean = jnp.where(some, summed / jnp.where(some, total, 1.0), 0.0)
    logs = jnp.where(some, top + jnp.log(jnp.where(some, total, 1.0)), NEG)
    place = OWN[slot]
    columns = slice(t * HEAD_DIM, (t + 1) * HEAD_DIM)
    if place < GROUP:
        u_ref[place, :, columns] = mean
    else:
        halo_ref[place - GROUP, :, columns] = mean.astype(jnp.bfloat16)
    log_ref[place, t] = jnp.transpose(logs)[:8]


def whole_kernel(
    nblocks, heads, bias, used, k, av, q, vv, video_proj, audio_proj,
    video_out, audio_out, bad_out,
    k_buf, av_buf, q_buf, vv_buf, o_ref, u_ref, halo_ref, log_ref, bad_ref,
    avx, vvx, u_acc, video_attn, audio_attn, wide_video, wide_audio,
    away_video, away_audio, there_video, there_audio, done, got, got_log, flag_out, flag_in,
    send, recv, local, zsend, zrecv, bsend, brecv, blocal, rsend, rrecv,
    weight, csend, crecv, fsend, frecv,
):
    me, place, base, plane, planes = where_am_i(nblocks)
    core = lax.axis_index("head")
    vid, aud = q.shape[0], k.shape[0]
    greet(place, base, plane, planes, core)
    arrays = ((k, k_buf, HALF), (av, av_buf, HALF), (q, q_buf, 0), (vv, vv_buf, 0))

    def column(member, t):
        return pl.ds(pl.multiple_of((member * heads + t) * HEAD_DIM, HEAD_DIM), HEAD_DIM)

    def arrival(t, n, d):
        src, dst, at = arrays[n]
        peer = place ^ d
        return remote(
            src.at[:, column(peer, t)], dst.at[t, place + at], send.at[t, n, d], recv.at[t, n, d], base + peer
        )

    own = {}
    for t in range(heads):
        for group in ((0, 1), (2, 3)):
            for d in (1, 2, 3):
                for n in group:
                    arrival(t, n, d).start()
    for t in range(heads):
        for n, (src, dst, at) in enumerate(arrays):
            own[t, n] = pltpu.make_async_copy(src.at[:, column(place, t)], dst.at[t, place + at], local.at[t, n])
            own[t, n].start()

    loads = [
        pltpu.make_async_copy(src, dst, weight.at[n])
        for n, (src, dst) in enumerate(((video_proj, wide_video), (audio_proj, wide_audio)))
    ]
    for load in loads:
        load.start()

    def returns(t, up):
        source, target = (HALF, 0) if up else (0, HALF)
        side = 0 if up else 1
        columns = slice(t * HEAD_DIM, (t + 1) * HEAD_DIM)
        pairs = (
            (halo_ref.at[pl.ds(source, HALF), :, columns], got.at[pl.ds(target, HALF), :, columns]),
            (log_ref.at[pl.ds(GROUP + source, HALF), t], got_log.at[pl.ds(target, HALF), t]),
        )
        return [
            remote(src, dst, rsend.at[t, side, n], rrecv.at[t, side, n], me + GROUP if up else me - GROUP)
            for n, (src, dst) in enumerate(pairs)
        ]

    results = ((o_ref, video_attn), (done, audio_attn))

    def back_copy(n, t, d):
        src, dst = results[n]
        peer = place ^ d
        return remote(
            src.at[peer, :, pl.ds(t * HEAD_DIM, HEAD_DIM)],
            dst.at[:, column(place, t)],
            bsend.at[n, t, d],
            brecv.at[n, t, d],
            base + peer,
        )

    def stay_copy(n, t):
        src, dst = results[n]
        return pltpu.make_async_copy(
            src.at[place, :, pl.ds(t * HEAD_DIM, HEAD_DIM)], dst.at[:, column(place, t)], blocal.at[n, t]
        )

    def wait_back(n):
        for t in range(heads):
            stay_copy(n, t).wait()
            for d in range(1, GROUP):
                back_copy(n, t, d).wait_recv()

    def finish_audio(t):
        @pl.when(plane > 0)
        def _():
            for copy in returns(t, True):
                copy.wait_recv()

        @pl.when(plane < planes - 1)
        def _():
            for copy in returns(t, False):
                copy.wait_recv()

        columns = slice(t * HEAD_DIM, (t + 1) * HEAD_DIM)
        for slot in range(GROUP):
            first, second = log_ref[slot, t], got_log[slot, t]
            top = jnp.maximum(first, second)
            a, b = jnp.exp(first - top), jnp.exp(second - top)
            share = a / (a + b)
            share = jnp.transpose(jnp.concatenate([share] * (HEAD_DIM // 8), axis=0))
            there = got[slot, :, columns].astype(jnp.float32)
            done[slot, :, columns] = (there + share * (u_ref[slot, :, columns] - there)).astype(jnp.bfloat16)
        stay_copy(1, t).start()
        for d in (3, 1, 2):
            back_copy(1, t, d).start()

    def relays(t, up):
        source, target = (GROUP, 0) if up else (HALF, GROUP + HALF)
        side = 0 if up else 1
        return [
            remote(
                x.at[t, pl.ds(source, HALF)],
                x.at[t, pl.ds(target, HALF)],
                zsend.at[t, side, n],
                zrecv.at[t, side, n],
                me + GROUP if up else me - GROUP,
            )
            for n, x in enumerate((k_buf, av_buf))
        ]

    avx[:, :, HEAD_DIM:] = jnp.ones((SLOTS, aud, HEAD_DIM), jnp.bfloat16)
    vvx[:, :, HEAD_DIM:] = jnp.ones((GROUP, vid, HEAD_DIM), jnp.bfloat16)

    @pl.when(plane == 0)
    def _():
        for x in (k_buf, av_buf):
            x[:, :HALF] = jnp.zeros((heads, HALF, aud, HEAD_DIM), jnp.bfloat16)

    @pl.when(plane == planes - 1)
    def _():
        for x in (k_buf, av_buf):
            x[:, GROUP + HALF :] = jnp.zeros((heads, HALF, aud, HEAD_DIM), jnp.bfloat16)

    def outside(total):
        wrong = jnp.where((total >= LOW) & (total <= HIGH), 0.0, 1.0)
        return jnp.max(wrong.reshape(-1, 8, HEAD_DIM), axis=0)

    @pl.when(plane == 0)
    def _():
        got[:HALF] = jnp.zeros((HALF,) + got.shape[1:], jnp.bfloat16)
        got_log[:HALF] = jnp.full((HALF,) + got_log.shape[1:], NEG, jnp.float32)

    @pl.when(plane == planes - 1)
    def _():
        got[HALF:] = jnp.zeros((HALF,) + got.shape[1:], jnp.bfloat16)
        got_log[HALF:] = jnp.full((HALF,) + got_log.shape[1:], NEG, jnp.float32)

    bad_ref[...] = jnp.zeros_like(bad_ref)
    for t in range(heads):
        for n in range(2):
            own[t, n].wait()
            for d in range(1, GROUP):
                arrival(t, n, d).wait_recv()

        @pl.when(plane < planes - 1)
        def _():
            for copy in relays(t, True):
                copy.start()

        @pl.when(plane > 0)
        def _():
            for copy in relays(t, False):
                copy.start()

        @pl.when(plane < planes - 1)
        def _():
            for copy in relays(t, False):
                copy.wait_recv()

        @pl.when(plane > 0)
        def _():
            for copy in relays(t, True):
                copy.wait_recv()

        avx[:, :, :HEAD_DIM] = av_buf[t]
        u_acc[...] = jnp.zeros_like(u_acc)
        columns = slice(t * HEAD_DIM, (t + 1) * HEAD_DIM)

        def step(d, carry):
            row = place ^ d

            @pl.when(d == 0)
            def _():
                own[t, 2].wait()
                own[t, 3].wait()

            @pl.when(d > 0)
            def _():
                arrival(t, 2, d).wait_recv()
                arrival(t, 3, d).wait_recv()

            vvx[row, :, :HEAD_DIM] = vv_buf[t, row]
            query = q_buf[t, row]
            weights = jnp.concatenate(
                [
                    jnp.exp2(
                        dot_t(query, k_buf[t, row + c]) * (SCALE * LOG2E) + bias[row * SPAN + c]
                    ).astype(jnp.bfloat16)
                    for c in range(SPAN)
                ],
                axis=1,
            )
            values = avx[pl.ds(row, SPAN)].reshape(SPAN * aud, 2 * HEAD_DIM)
            out = jnp.dot(weights, values, preferred_element_type=jnp.float32)
            total = out[:, HEAD_DIM:]
            o_ref[row, :, columns] = (out[:, :HEAD_DIM] / total).astype(jnp.bfloat16)
            bad_ref[...] = jnp.maximum(bad_ref[...], outside(total))
            back = lax.dot_general(
                weights, vvx[row], (((0,), (0,)), ((), ())), preferred_element_type=jnp.float32
            )
            u_acc[pl.ds(row, SPAN)] += back.reshape(SPAN, aud, 2 * HEAD_DIM)

            @pl.when(d == 0)
            def _():
                stay_copy(0, t).start()

            @pl.when(d > 0)
            def _():
                back_copy(0, t, d).start()

            return carry

        lax.fori_loop(0, GROUP, step, 0)
        for slot in range(SLOTS):
            total = u_acc[slot, :, HEAD_DIM:]
            bad_ref[...] = jnp.maximum(bad_ref[...], outside(total) * used[slot])
            write_audio(t, slot, total, u_acc[slot, :, :HEAD_DIM], 0.0, u_ref, halo_ref, log_ref)
        @pl.when(plane < planes - 1)
        def _():
            for copy in returns(t, True):
                copy.start()

        @pl.when(plane > 0)
        def _():
            for copy in returns(t, False):
                copy.start()

        if t > 0:
            finish_audio(t - 1)

    def flags(stage):
        lines = [{"seq": lax.rem(plane + e, planes) * GROUP + place} for e in range(1, planes)]
        peers = [{"seq": base + (place ^ d)} for d in range(1, GROUP)]
        at, targets = ((0, lines), (planes - 1, peers), (planes + GROUP - 2, [{"head": 1 - core}]))[stage]
        return at, [
            pltpu.make_async_remote_copy(
                src_ref=flag_out.at[stage],
                dst_ref=flag_in.at[at + n],
                send_sem=fsend.at[at + n],
                recv_sem=frecv.at[at + n],
                device_id=target,
                device_id_type=LOGICAL,
            )
            for n, target in enumerate(targets)
        ]

    def start_flags(stage):
        flag_out[stage] = bad_ref[...]
        for copy in flags(stage)[1]:
            copy.start()

    def end_flags(stage):
        at, sent = flags(stage)
        for n, copy in enumerate(sent):
            copy.wait()
            bad_ref[...] = jnp.maximum(bad_ref[...], flag_in[at + n])

    start_flags(0)
    finish_audio(heads - 1)
    half = video_out.shape[1]
    tiles = half // TILE

    def columns_of(who, tile):
        return pl.ds(pl.multiple_of(who * half + tile * TILE, TILE), TILE)

    def project(n, attn, weights, away, there, out):
        def passing(tile):
            columns = pl.ds(pl.multiple_of(tile * TILE, TILE), TILE)
            return pltpu.make_async_remote_copy(
                src_ref=away.at[:, columns],
                dst_ref=there.at[:, columns],
                send_sem=csend.at[n, tile],
                recv_sem=crecv.at[n, tile],
                device_id={"head": 1 - core},
                device_id_type=LOGICAL,
            )

        def theirs(tile, carry):
            away[:, pl.ds(pl.multiple_of(tile * TILE, TILE), TILE)] = jnp.dot(
                attn[...], weights[:, columns_of(1 - core, tile)], preferred_element_type=jnp.float32
            )
            passing(tile).start()
            return carry

        def mine(tile, carry):
            columns = pl.ds(pl.multiple_of(tile * TILE, TILE), TILE)
            part = jnp.dot(attn[...], weights[:, columns_of(core, tile)], preferred_element_type=jnp.float32)
            passing(tile).wait_recv()
            out[:, columns] = (part + there[:, columns]).astype(jnp.bfloat16)
            passing(tile).wait_send()
            return carry

        lax.fori_loop(0, tiles, theirs, 0)
        lax.fori_loop(0, tiles, mine, 0)

    end_flags(0)
    start_flags(1)
    loads[0].wait()
    wait_back(0)
    project(0, video_attn, wide_video, away_video, there_video, video_out)
    end_flags(1)
    start_flags(2)
    loads[1].wait()
    wait_back(1)
    project(1, audio_attn, wide_audio, away_audio, there_audio, audio_out)
    end_flags(2)
    bad_out[0] = jnp.max(bad_ref[...])
    for t in range(heads):
        for d in range(1, GROUP):
            for n in range(4):
                arrival(t, n, d).wait_send()
            for n in range(2):
                back_copy(n, t, d).wait_send()

    @pl.when(plane < planes - 1)
    def _():
        for t in range(heads):
            for copy in relays(t, True) + returns(t, True):
                copy.wait_send()

    @pl.when(plane > 0)
    def _():
        for t in range(heads):
            for copy in relays(t, False) + returns(t, False):
                copy.wait_send()


def whole_call(bias, used, k, av, q, vv, video_proj, audio_proj, nblocks):
    vid, aud = q.shape[0], k.shape[0]
    heads = q.shape[1] // HEAD_DIM // GROUP
    width = heads * HEAD_DIM
    wide = 2 * HEAD_DIM
    half = video_proj.shape[1] // 2
    planes = nblocks // GROUP
    messages = planes - 1 + GROUP
    anyspace = pl.BlockSpec(memory_space=pl.ANY)
    smem = pl.BlockSpec(memory_space=pltpu.SMEM)
    vmem = pl.BlockSpec(memory_space=pltpu.VMEM)
    bf16, f32, dma = jnp.bfloat16, jnp.float32, pltpu.SemaphoreType.DMA
    return pl.pallas_call(
        lambda *refs: whole_kernel(nblocks, heads, *refs),
        in_specs=[smem, smem] + [anyspace] * 6,
        out_specs=[vmem, vmem, smem],
        out_shape=[
            jax.ShapeDtypeStruct((vid, half), bf16),
            jax.ShapeDtypeStruct((aud, half), bf16),
            jax.ShapeDtypeStruct((1,), f32),
        ],
        scratch_shapes=[
            pltpu.VMEM((heads, SLOTS, aud, HEAD_DIM), bf16),
            pltpu.VMEM((heads, SLOTS, aud, HEAD_DIM), bf16),
            pltpu.VMEM((heads, GROUP, vid, HEAD_DIM), bf16),
            pltpu.VMEM((heads, GROUP, vid, HEAD_DIM), bf16),
            pltpu.VMEM((GROUP, vid, width), bf16),
            pltpu.VMEM((GROUP, aud, width), f32),
            pltpu.VMEM((GROUP, aud, width), bf16),
            pltpu.VMEM((SLOTS, heads, 8, aud), f32),
            pltpu.VMEM((8, HEAD_DIM), f32),
            pltpu.VMEM((SLOTS, aud, wide), bf16),
            pltpu.VMEM((GROUP, vid, wide), bf16),
            pltpu.VMEM((SLOTS, aud, wide), f32),
            pltpu.VMEM((vid, GROUP * width), bf16),
            pltpu.VMEM((aud, GROUP * width), bf16),
            pltpu.VMEM(video_proj.shape, bf16),
            pltpu.VMEM(audio_proj.shape, bf16),
            pltpu.VMEM((vid, half), f32),
            pltpu.VMEM((aud, half), f32),
            pltpu.VMEM((vid, half), f32),
            pltpu.VMEM((aud, half), f32),
            pltpu.VMEM((GROUP, aud, width), bf16),
            pltpu.VMEM((GROUP, aud, width), bf16),
            pltpu.VMEM((GROUP, heads, 8, aud), f32),
            pltpu.VMEM((3, 8, HEAD_DIM), f32),
            pltpu.VMEM((messages, 8, HEAD_DIM), f32),
            dma((heads, 4, GROUP)),
            dma((heads, 4, GROUP)),
            dma((heads, 4)),
            dma((heads, 2, 2)),
            dma((heads, 2, 2)),
            dma((2, heads, GROUP)),
            dma((2, heads, GROUP)),
            dma((2, heads)),
            dma((heads, 2, 2)),
            dma((heads, 2, 2)),
            dma((2,)),
            dma((2, half // TILE)),
            dma((2, half // TILE)),
            dma((messages,)),
            dma((messages,)),
        ],
        compiler_params=pltpu.CompilerParams(
            collective_id=0, has_side_effects=True, vmem_limit_bytes=60 * 1024 * 1024
        ),
    )(bias, used, k, av, q, vv, video_proj, audio_proj)


def shards(
    video_query, video_value, audio_key, audio_value, video_proj, audio_proj, pair_first, pair_count
):
    nblocks = lax.axis_size("seq")
    me = lax.axis_index("seq")
    base = me - me % GROUP
    offsets = jnp.arange(SPAN)[None, :] - HALF + base + jnp.arange(GROUP)[:, None]
    first = lax.dynamic_slice_in_dim(pair_first, base, GROUP)[:, None]
    count = lax.dynamic_slice_in_dim(pair_count, base, GROUP)[:, None]
    valid = (offsets >= first) & (offsets < first + count)
    bias = jnp.where(valid, 0.0, NEG).astype(jnp.float32).reshape(-1)
    audio_blocks = base - HALF + jnp.arange(SLOTS)[None, :]
    used = jnp.any((audio_blocks >= first) & (audio_blocks < first + count), axis=0).astype(jnp.float32)
    video_out, audio_out, bad = whole_call(
        bias, used, audio_key, audio_value, video_query, video_value, video_proj, audio_proj, nblocks
    )
    arguments = (
        video_query, video_value, audio_key, audio_value, video_proj, audio_proj, pair_first, pair_count
    )
    return lax.cond(
        bad[0] > 0, lambda: safe_shards(*arguments), lambda: (video_out, audio_out)
    )


def solution(mesh):
    in_specs = (
        P("seq", "head"),
        P("seq", "head"),
        P("seq", "head"),
        P("seq", "head"),
        P("head", None),
        P("head", None),
        P(),
        P(),
    )
    out_specs = (P("seq", "head"), P("seq", "head"))
    return jax.shard_map(shards, mesh=mesh, in_specs=in_specs, out_specs=out_specs, check_vma=False)
```

```python
import math

import jax
import jax.numpy as jnp
from jax import lax
from jax.experimental import pallas as pl
from jax.experimental.pallas import tpu as pltpu
from jax.sharding import PartitionSpec as P

HEAD_DIM = 128
GROUP = 4
HALF = 2
NEG = -1e30
SCALE = 1.0 / math.sqrt(HEAD_DIM)
LOG2E = 1.4426950408889634
LOW, HIGH = 1e-25, 1e25
LOGICAL = pl.DeviceIdType.MESH


def shifted(x, axis, by):
    size = lax.axis_size(axis)
    pairs = [(i, i + by) for i in range(size) if 0 <= i + by < size]
    return lax.ppermute(x, axis, pairs)


def tile_scores(query, keys):
    return jnp.einsum("vhe,ahe->hva", query, keys, preferred_element_type=jnp.float32) / math.sqrt(
        HEAD_DIM
    )


def row_piece(scores, values):
    top = jnp.max(scores, axis=2)
    expo = jnp.exp(scores - top[:, :, None])
    total = jnp.sum(expo, axis=2)
    out = jnp.einsum(
        "hva,ahe->vhe", expo.astype(jnp.bfloat16), values, preferred_element_type=jnp.float32
    )
    return (top, total, out)


def col_piece(scores, values):
    top = jnp.max(scores, axis=1)
    expo = jnp.exp(scores - top[:, None, :])
    total = jnp.sum(expo, axis=1)
    out = jnp.einsum(
        "hva,vhe->ahe", expo.astype(jnp.bfloat16), values, preferred_element_type=jnp.float32
    )
    return (top, total, out)


def combine(acc, part):
    top_a, total_a, out_a = acc
    top_b, total_b, out_b = part
    top = jnp.maximum(top_a, top_b)
    old = jnp.exp(top_a - top)
    new = jnp.exp(top_b - top)
    return (
        top,
        total_a * old + total_b * new,
        out_a * old.T[:, :, None] + out_b * new.T[:, :, None],
    )


def empty_acc(heads, rows):
    return (
        jnp.full((heads, rows), NEG, jnp.float32),
        jnp.zeros((heads, rows), jnp.float32),
        jnp.zeros((rows, heads, HEAD_DIM), jnp.float32),
    )


def finish(acc):
    top, total, out = acc
    result = (out / total.T[:, :, None]).astype(jnp.bfloat16)
    return result.reshape(result.shape[0], result.shape[1] * result.shape[2])


def safe_shards(
    video_query, video_value, audio_key, audio_value, video_proj, audio_proj, pair_first, pair_count
):
    heads = video_query.shape[1] // HEAD_DIM
    vid = video_query.shape[0]
    aud = audio_key.shape[0]
    nblocks = lax.axis_size("seq")
    me = lax.axis_index("seq")
    first = pair_first[me]
    count = pair_count[me]
    query = video_query.reshape(vid, heads, HEAD_DIM)
    own_keys = audio_key.reshape(aud, heads, HEAD_DIM)
    audio_pair = jnp.stack([audio_key, audio_value])
    video_pair = jnp.stack([video_query, video_value])
    video_acc = empty_acc(heads, vid)
    audio_acc = empty_acc(heads, aud)
    for offset in range(-HALF, HALF + 1):
        if offset == 0:
            arrived = audio_pair
        else:
            arrived = shifted(audio_pair, "seq", -offset)
        keys = arrived[0].reshape(aud, heads, HEAD_DIM)
        aud_vals = arrived[1].reshape(aud, heads, HEAD_DIM)
        target = me + offset
        valid = (target >= first) & (target < first + count)
        source = me - offset
        clipped = jnp.clip(source, 0, nblocks - 1)
        from_source = (
            (source >= 0)
            & (source < nblocks)
            & (pair_first[clipped] <= me)
            & (me < pair_first[clipped] + pair_count[clipped])
        )

        def video_side(unused):
            return row_piece(tile_scores(query, keys), aud_vals)

        def no_video(unused):
            return empty_acc(heads, vid)

        video_acc = combine(video_acc, lax.cond(valid, video_side, no_video, 0))
        if offset == 0:
            visiting = video_pair
        else:
            visiting = shifted(video_pair, "seq", offset)

        def audio_side(unused):
            visit_query = visiting[0].reshape(vid, heads, HEAD_DIM)
            visit_vals = visiting[1].reshape(vid, heads, HEAD_DIM)
            return col_piece(tile_scores(visit_query, own_keys), visit_vals)

        def no_audio(unused):
            return empty_acc(heads, aud)

        audio_acc = combine(audio_acc, lax.cond(from_source, audio_side, no_audio, 0))
    video_attn = finish(video_acc)
    audio_attn = finish(audio_acc)
    video_term = jnp.dot(video_attn, video_proj, preferred_element_type=jnp.float32)
    audio_term = jnp.dot(audio_attn, audio_proj, preferred_element_type=jnp.float32)
    half = video_proj.shape[1] // 2
    core = lax.axis_index("head")

    def total(term):
        away = lax.dynamic_slice_in_dim(term, (1 - core) * half, half, 1)
        mine = lax.dynamic_slice_in_dim(term, core * half, half, 1)
        return (mine + lax.ppermute(away, "head", [(0, 1), (1, 0)])).astype(jnp.bfloat16)

    return (total(video_term), total(audio_term))


def greet(place, base, plane, planes, core):
    barrier = pltpu.get_barrier_semaphore()
    for d in range(1, GROUP):
        pl.semaphore_signal(barrier, inc=1, device_id={"seq": base + (place ^ d)}, device_id_type=LOGICAL)
    for e in range(1, planes):
        target = lax.rem(plane + e, planes) * GROUP + place
        pl.semaphore_signal(barrier, inc=1, device_id={"seq": target}, device_id_type=LOGICAL)
    pl.semaphore_signal(barrier, inc=1, device_id={"head": 1 - core}, device_id_type=LOGICAL)
    pl.semaphore_wait(barrier, GROUP + planes - 1)


def where_am_i(nblocks):
    me = lax.axis_index("seq")
    place = lax.rem(me, GROUP)
    return me, place, me - place, me // GROUP, nblocks // GROUP


def remote(src, dst, send, recv, target):
    return pltpu.make_async_remote_copy(
        src_ref=src, dst_ref=dst, send_sem=send, recv_sem=recv, device_id={"seq": target}, device_id_type=LOGICAL
    )


TILE = 512
SPAN = 2 * HALF + 1
SLOTS = GROUP + 2 * HALF
OWN = (4, 5, 0, 1, 2, 3, 6, 7)


def dot_t(a, b):
    return lax.dot_general(a, b, (((1,), (1,)), ((), ())), preferred_element_type=jnp.float32)


def write_audio(t, slot, total, summed, top, u_ref, halo_ref, log_ref):
    some = total > 0
    mean = jnp.where(some, summed / jnp.where(some, total, 1.0), 0.0)
    logs = jnp.where(some, top + jnp.log(jnp.where(some, total, 1.0)), NEG)
    place = OWN[slot]
    columns = slice(t * HEAD_DIM, (t + 1) * HEAD_DIM)
    if place < GROUP:
        u_ref[place, :, columns] = mean
    else:
        halo_ref[place - GROUP, :, columns] = mean.astype(jnp.bfloat16)
    log_ref[place, t] = jnp.transpose(logs)[:8]


def whole_kernel(
    nblocks, heads, bias, used, k, av, q, vv, video_proj, audio_proj,
    video_out, audio_out, bad_out,
    k_buf, av_buf, q_buf, vv_buf, o_ref, u_ref, halo_ref, log_ref, bad_ref,
    avx, vvx, u_acc, video_attn, audio_attn, wide_video, wide_audio,
    away_video, away_audio, there_video, there_audio, done, got, got_log, flag_out, flag_in,
    send, recv, local, zsend, zrecv, bsend, brecv, blocal, rsend, rrecv,
    weight, csend, crecv, fsend, frecv,
):
    me, place, base, plane, planes = where_am_i(nblocks)
    core = lax.axis_index("head")
    vid, aud = q.shape[0], k.shape[0]
    greet(place, base, plane, planes, core)
    arrays = ((k, k_buf, HALF), (av, av_buf, HALF), (q, q_buf, 0), (vv, vv_buf, 0))

    def column(member, t):
        return pl.ds(pl.multiple_of((member * heads + t) * HEAD_DIM, HEAD_DIM), HEAD_DIM)

    def arrival(t, n, d):
        src, dst, at = arrays[n]
        peer = place ^ d
        return remote(
            src.at[:, column(peer, t)], dst.at[t, place + at], send.at[t, n, d], recv.at[t, n, d], base + peer
        )

    own = {}
    for t in range(heads):
        for group in ((0, 1), (2, 3)):
            for d in (1, 2, 3):
                for n in group:
                    arrival(t, n, d).start()
    for t in range(heads):
        for n, (src, dst, at) in enumerate(arrays):
            own[t, n] = pltpu.make_async_copy(src.at[:, column(place, t)], dst.at[t, place + at], local.at[t, n])
            own[t, n].start()

    loads = [
        pltpu.make_async_copy(src, dst, weight.at[n])
        for n, (src, dst) in enumerate(((video_proj, wide_video), (audio_proj, wide_audio)))
    ]
    for load in loads:
        load.start()

    def returns(t, up):
        source, target = (HALF, 0) if up else (0, HALF)
        side = 0 if up else 1
        columns = slice(t * HEAD_DIM, (t + 1) * HEAD_DIM)
        pairs = (
            (halo_ref.at[pl.ds(source, HALF), :, columns], got.at[pl.ds(target, HALF), :, columns]),
            (log_ref.at[pl.ds(GROUP + source, HALF), t], got_log.at[pl.ds(target, HALF), t]),
        )
        return [
            remote(src, dst, rsend.at[t, side, n], rrecv.at[t, side, n], me + GROUP if up else me - GROUP)
            for n, (src, dst) in enumerate(pairs)
        ]

    results = ((o_ref, video_attn), (done, audio_attn))

    def back_copy(n, t, d):
        src, dst = results[n]
        peer = place ^ d
        return remote(
            src.at[peer, :, pl.ds(t * HEAD_DIM, HEAD_DIM)],
            dst.at[:, column(place, t)],
            bsend.at[n, t, d],
            brecv.at[n, t, d],
            base + peer,
        )

    def stay_copy(n, t):
        src, dst = results[n]
        return pltpu.make_async_copy(
            src.at[place, :, pl.ds(t * HEAD_DIM, HEAD_DIM)], dst.at[:, column(place, t)], blocal.at[n, t]
        )

    def wait_back(n):
        for t in range(heads):
            stay_copy(n, t).wait()
            for d in range(1, GROUP):
                back_copy(n, t, d).wait_recv()

    def finish_audio(t):
        @pl.when(plane > 0)
        def _():
            for copy in returns(t, True):
                copy.wait_recv()

        @pl.when(plane < planes - 1)
        def _():
            for copy in returns(t, False):
                copy.wait_recv()

        columns = slice(t * HEAD_DIM, (t + 1) * HEAD_DIM)
        for slot in range(GROUP):
            first, second = log_ref[slot, t], got_log[slot, t]
            top = jnp.maximum(first, second)
            a, b = jnp.exp(first - top), jnp.exp(second - top)
            share = a / (a + b)
            share = jnp.transpose(jnp.concatenate([share] * (HEAD_DIM // 8), axis=0))
            there = got[slot, :, columns].astype(jnp.float32)
            done[slot, :, columns] = (there + share * (u_ref[slot, :, columns] - there)).astype(jnp.bfloat16)
        stay_copy(1, t).start()
        for d in (3, 1, 2):
            back_copy(1, t, d).start()

    def relays(t, up):
        source, target = (GROUP, 0) if up else (HALF, GROUP + HALF)
        side = 0 if up else 1
        return [
            remote(
                x.at[t, pl.ds(source, HALF)],
                x.at[t, pl.ds(target, HALF)],
                zsend.at[t, side, n],
                zrecv.at[t, side, n],
                me + GROUP if up else me - GROUP,
            )
            for n, x in enumerate((k_buf, av_buf))
        ]

    avx[:, :, HEAD_DIM:] = jnp.ones((SLOTS, aud, HEAD_DIM), jnp.bfloat16)
    vvx[:, :, HEAD_DIM:] = jnp.ones((GROUP, vid, HEAD_DIM), jnp.bfloat16)

    @pl.when(plane == 0)
    def _():
        for x in (k_buf, av_buf):
            x[:, :HALF] = jnp.zeros((heads, HALF, aud, HEAD_DIM), jnp.bfloat16)

    @pl.when(plane == planes - 1)
    def _():
        for x in (k_buf, av_buf):
            x[:, GROUP + HALF :] = jnp.zeros((heads, HALF, aud, HEAD_DIM), jnp.bfloat16)

    def outside(total):
        wrong = jnp.where((total >= LOW) & (total <= HIGH), 0.0, 1.0)
        return jnp.max(wrong.reshape(-1, 8, HEAD_DIM), axis=0)

    @pl.when(plane == 0)
    def _():
        got[:HALF] = jnp.zeros((HALF,) + got.shape[1:], jnp.bfloat16)
        got_log[:HALF] = jnp.full((HALF,) + got_log.shape[1:], NEG, jnp.float32)

    @pl.when(plane == planes - 1)
    def _():
        got[HALF:] = jnp.zeros((HALF,) + got.shape[1:], jnp.bfloat16)
        got_log[HALF:] = jnp.full((HALF,) + got_log.shape[1:], NEG, jnp.float32)

    bad_ref[...] = jnp.zeros_like(bad_ref)
    for t in range(heads):
        for n in range(2):
            own[t, n].wait()
            for d in range(1, GROUP):
                arrival(t, n, d).wait_recv()

        @pl.when(plane < planes - 1)
        def _():
            for copy in relays(t, True):
                copy.start()

        @pl.when(plane > 0)
        def _():
            for copy in relays(t, False):
                copy.start()

        @pl.when(plane < planes - 1)
        def _():
            for copy in relays(t, False):
                copy.wait_recv()

        @pl.when(plane > 0)
        def _():
            for copy in relays(t, True):
                copy.wait_recv()

        avx[:, :, :HEAD_DIM] = av_buf[t]
        u_acc[...] = jnp.zeros_like(u_acc)
        columns = slice(t * HEAD_DIM, (t + 1) * HEAD_DIM)

        def step(d, carry):
            row = place ^ d

            @pl.when(d == 0)
            def _():
                own[t, 2].wait()
                own[t, 3].wait()

            @pl.when(d > 0)
            def _():
                arrival(t, 2, d).wait_recv()
                arrival(t, 3, d).wait_recv()
                if t == heads - 1:
                    for e in range(heads - 1):
                        back_copy(0, e, d).start()

            vvx[row, :, :HEAD_DIM] = vv_buf[t, row]
            query = q_buf[t, row]
            weights = jnp.concatenate(
                [
                    jnp.exp2(
                        dot_t(query, k_buf[t, row + c]) * (SCALE * LOG2E) + bias[row * SPAN + c]
                    ).astype(jnp.bfloat16)
                    for c in range(SPAN)
                ],
                axis=1,
            )
            values = avx[pl.ds(row, SPAN)].reshape(SPAN * aud, 2 * HEAD_DIM)
            out = jnp.dot(weights, values, preferred_element_type=jnp.float32)
            total = out[:, HEAD_DIM:]
            o_ref[row, :, columns] = (out[:, :HEAD_DIM] / total).astype(jnp.bfloat16)
            bad_ref[...] = jnp.maximum(bad_ref[...], outside(total))
            back = lax.dot_general(
                weights, vvx[row], (((0,), (0,)), ((), ())), preferred_element_type=jnp.float32
            )
            u_acc[pl.ds(row, SPAN)] += back.reshape(SPAN, aud, 2 * HEAD_DIM)

            @pl.when(d == 0)
            def _():
                stay_copy(0, t).start()

            if t == heads - 1:

                @pl.when(d > 0)
                def _():
                    back_copy(0, t, d).start()

            return carry

        lax.fori_loop(0, GROUP, step, 0)
        for slot in range(SLOTS):
            total = u_acc[slot, :, HEAD_DIM:]
            bad_ref[...] = jnp.maximum(bad_ref[...], outside(total) * used[slot])
            write_audio(t, slot, total, u_acc[slot, :, :HEAD_DIM], 0.0, u_ref, halo_ref, log_ref)
        @pl.when(plane < planes - 1)
        def _():
            for copy in returns(t, True):
                copy.start()

        @pl.when(plane > 0)
        def _():
            for copy in returns(t, False):
                copy.start()

        if t == heads - 1:
            for e in range(heads - 1):
                finish_audio(e)

    def flags(stage):
        lines = [{"seq": lax.rem(plane + e, planes) * GROUP + place} for e in range(1, planes)]
        peers = [{"seq": base + (place ^ d)} for d in range(1, GROUP)]
        at, targets = ((0, lines), (planes - 1, peers), (planes + GROUP - 2, [{"head": 1 - core}]))[stage]
        return at, [
            pltpu.make_async_remote_copy(
                src_ref=flag_out.at[stage],
                dst_ref=flag_in.at[at + n],
                send_sem=fsend.at[at + n],
                recv_sem=frecv.at[at + n],
                device_id=target,
                device_id_type=LOGICAL,
            )
            for n, target in enumerate(targets)
        ]

    def start_flags(stage):
        flag_out[stage] = bad_ref[...]
        for copy in flags(stage)[1]:
            copy.start()

    def end_flags(stage):
        at, sent = flags(stage)
        for n, copy in enumerate(sent):
            copy.wait()
            bad_ref[...] = jnp.maximum(bad_ref[...], flag_in[at + n])

    start_flags(0)
    finish_audio(heads - 1)
    half = video_out.shape[1]
    tiles = half // TILE

    def columns_of(who, tile):
        return pl.ds(pl.multiple_of(who * half + tile * TILE, TILE), TILE)

    def project(n, attn, weights, away, there, out):
        def passing(tile):
            columns = pl.ds(pl.multiple_of(tile * TILE, TILE), TILE)
            return pltpu.make_async_remote_copy(
                src_ref=away.at[:, columns],
                dst_ref=there.at[:, columns],
                send_sem=csend.at[n, tile],
                recv_sem=crecv.at[n, tile],
                device_id={"head": 1 - core},
                device_id_type=LOGICAL,
            )

        def theirs(tile, carry):
            away[:, pl.ds(pl.multiple_of(tile * TILE, TILE), TILE)] = jnp.dot(
                attn[...], weights[:, columns_of(1 - core, tile)], preferred_element_type=jnp.float32
            )
            passing(tile).start()
            return carry

        def mine(tile, carry):
            columns = pl.ds(pl.multiple_of(tile * TILE, TILE), TILE)
            part = jnp.dot(attn[...], weights[:, columns_of(core, tile)], preferred_element_type=jnp.float32)
            passing(tile).wait_recv()
            out[:, columns] = (part + there[:, columns]).astype(jnp.bfloat16)
            passing(tile).wait_send()
            return carry

        lax.fori_loop(0, tiles, theirs, 0)
        lax.fori_loop(0, tiles, mine, 0)

    end_flags(0)
    start_flags(1)
    loads[0].wait()
    wait_back(0)
    project(0, video_attn, wide_video, away_video, there_video, video_out)
    end_flags(1)
    start_flags(2)
    loads[1].wait()
    wait_back(1)
    project(1, audio_attn, wide_audio, away_audio, there_audio, audio_out)
    end_flags(2)
    bad_out[0] = jnp.max(bad_ref[...])
    for t in range(heads):
        for d in range(1, GROUP):
            for n in range(4):
                arrival(t, n, d).wait_send()
            for n in range(2):
                back_copy(n, t, d).wait_send()

    @pl.when(plane < planes - 1)
    def _():
        for t in range(heads):
            for copy in relays(t, True) + returns(t, True):
                copy.wait_send()

    @pl.when(plane > 0)
    def _():
        for t in range(heads):
            for copy in relays(t, False) + returns(t, False):
                copy.wait_send()


def whole_call(bias, used, k, av, q, vv, video_proj, audio_proj, nblocks):
    vid, aud = q.shape[0], k.shape[0]
    heads = q.shape[1] // HEAD_DIM // GROUP
    width = heads * HEAD_DIM
    wide = 2 * HEAD_DIM
    half = video_proj.shape[1] // 2
    planes = nblocks // GROUP
    messages = planes - 1 + GROUP
    anyspace = pl.BlockSpec(memory_space=pl.ANY)
    smem = pl.BlockSpec(memory_space=pltpu.SMEM)
    vmem = pl.BlockSpec(memory_space=pltpu.VMEM)
    bf16, f32, dma = jnp.bfloat16, jnp.float32, pltpu.SemaphoreType.DMA
    return pl.pallas_call(
        lambda *refs: whole_kernel(nblocks, heads, *refs),
        in_specs=[smem, smem] + [anyspace] * 6,
        out_specs=[vmem, vmem, smem],
        out_shape=[
            jax.ShapeDtypeStruct((vid, half), bf16),
            jax.ShapeDtypeStruct((aud, half), bf16),
            jax.ShapeDtypeStruct((1,), f32),
        ],
        scratch_shapes=[
            pltpu.VMEM((heads, SLOTS, aud, HEAD_DIM), bf16),
            pltpu.VMEM((heads, SLOTS, aud, HEAD_DIM), bf16),
            pltpu.VMEM((heads, GROUP, vid, HEAD_DIM), bf16),
            pltpu.VMEM((heads, GROUP, vid, HEAD_DIM), bf16),
            pltpu.VMEM((GROUP, vid, width), bf16),
            pltpu.VMEM((GROUP, aud, width), f32),
            pltpu.VMEM((GROUP, aud, width), bf16),
            pltpu.VMEM((SLOTS, heads, 8, aud), f32),
            pltpu.VMEM((8, HEAD_DIM), f32),
            pltpu.VMEM((SLOTS, aud, wide), bf16),
            pltpu.VMEM((GROUP, vid, wide), bf16),
            pltpu.VMEM((SLOTS, aud, wide), f32),
            pltpu.VMEM((vid, GROUP * width), bf16),
            pltpu.VMEM((aud, GROUP * width), bf16),
            pltpu.VMEM(video_proj.shape, bf16),
            pltpu.VMEM(audio_proj.shape, bf16),
            pltpu.VMEM((vid, half), f32),
            pltpu.VMEM((aud, half), f32),
            pltpu.VMEM((vid, half), f32),
            pltpu.VMEM((aud, half), f32),
            pltpu.VMEM((GROUP, aud, width), bf16),
            pltpu.VMEM((GROUP, aud, width), bf16),
            pltpu.VMEM((GROUP, heads, 8, aud), f32),
            pltpu.VMEM((3, 8, HEAD_DIM), f32),
            pltpu.VMEM((messages, 8, HEAD_DIM), f32),
            dma((heads, 4, GROUP)),
            dma((heads, 4, GROUP)),
            dma((heads, 4)),
            dma((heads, 2, 2)),
            dma((heads, 2, 2)),
            dma((2, heads, GROUP)),
            dma((2, heads, GROUP)),
            dma((2, heads)),
            dma((heads, 2, 2)),
            dma((heads, 2, 2)),
            dma((2,)),
            dma((2, half // TILE)),
            dma((2, half // TILE)),
            dma((messages,)),
            dma((messages,)),
        ],
        compiler_params=pltpu.CompilerParams(
            collective_id=0, has_side_effects=True, vmem_limit_bytes=60 * 1024 * 1024
        ),
    )(bias, used, k, av, q, vv, video_proj, audio_proj)


def shards(
    video_query, video_value, audio_key, audio_value, video_proj, audio_proj, pair_first, pair_count
):
    nblocks = lax.axis_size("seq")
    me = lax.axis_index("seq")
    base = me - me % GROUP
    offsets = jnp.arange(SPAN)[None, :] - HALF + base + jnp.arange(GROUP)[:, None]
    first = lax.dynamic_slice_in_dim(pair_first, base, GROUP)[:, None]
    count = lax.dynamic_slice_in_dim(pair_count, base, GROUP)[:, None]
    valid = (offsets >= first) & (offsets < first + count)
    bias = jnp.where(valid, 0.0, NEG).astype(jnp.float32).reshape(-1)
    audio_blocks = base - HALF + jnp.arange(SLOTS)[None, :]
    used = jnp.any((audio_blocks >= first) & (audio_blocks < first + count), axis=0).astype(jnp.float32)
    video_out, audio_out, bad = whole_call(
        bias, used, audio_key, audio_value, video_query, video_value, video_proj, audio_proj, nblocks
    )
    arguments = (
        video_query, video_value, audio_key, audio_value, video_proj, audio_proj, pair_first, pair_count
    )
    return lax.cond(
        bad[0] > 0, lambda: safe_shards(*arguments), lambda: (video_out, audio_out)
    )


def solution(mesh):
    in_specs = (
        P("seq", "head"),
        P("seq", "head"),
        P("seq", "head"),
        P("seq", "head"),
        P("head", None),
        P("head", None),
        P(),
        P(),
    )
    out_specs = (P("seq", "head"), P("seq", "head"))
    return jax.shard_map(shards, mesh=mesh, in_specs=in_specs, out_specs=out_specs, check_vma=False)
```
